256 devices in a mesh: group: 4 (over z_hi), dom: 16 (over x, y), pen: 4 (over z_lo, core).
Axes of the slice: x: 4, y: 4, z: 8 (z_hi: 4, z_lo: 2; z = z_hi * 2 + z_lo), core: 2. Of those that a mesh axis runs over, the one named last changes fastest.
Arguments:
- atom_positions: float32 [64, 4, 3, 2048], P(('group', 'dom'), 'pen'), may hold values from 0 to 1
- atom_charges: float32 [64, 4, 2048], P(('group', 'dom'), 'pen'), may hold values from -1.2 to 1.2
- multipole_basis: float32 [64, 4, 4, 2048], P(('group', 'dom'), 'pen'), may hold values from -6 to 6
- spread_cell: int32 [64, 4, 8, 2048], P(('group', 'dom'), 'pen'), may hold values from 0 to 32767
- spread_weight: float32 [64, 4, 8, 2048], P(('group', 'dom'), 'pen'), may hold values from 0 to 0.25
- line_slab: int32 [64, 4, 256, 1], P(('group', 'dom'), 'pen'), may hold values from 0 to 63; in each aligned block of 256 rows (0 to 255, 256 to 511, ..., all dimensions but the last counted through in order) at most 8 rows name the same one
- line_target: int32 [64, 4, 256], P(('group', 'dom'), 'pen'), may hold values from 0 to 63
- neighbour_tiles: int32 [64, 4, 16, 16], P(('group', 'dom'), 'pen'), may hold values from 0 to 143
- live_tiles: int32 [64, 4], P(('group', 'dom'), 'pen'), may hold values from 1 to 16, as said below
- initial_density: float32 [128, 128, 128], P(('group', 'dom'), 'pen'), may hold values from -3 to 3
- susceptibility: float32 [128, 128, 128], P(('group', 'dom'), 'pen'), may hold values from 0.05 to 0.5
- ion_potential: float32 [128, 128, 128], P(('group', 'dom'), 'pen'), may hold values from -6 to 6
Outputs:
- potential: float32 [128, 128, 128], P(('group', 'dom'), 'pen')
- density: float32 [128, 128, 128], P(('group', 'dom'), 'pen')
- mm_potential: float32 [64, 4, 2048], P(('group', 'dom'), 'pen')
The draws below stay inside these ranges and needn't reach their ends.
Inputs may be any that keep to these rules, and one draw needn't show every extreme that they name: `live_tiles`: every domain has at least one live tile and some domain has all 16 live. `line_slab`: no grid slab is named by more than 8 of the 256 lines of one domain; in some domain one slab is named exactly 8 times.
All inputs are finite; a program needn't handle non-finite values.
Results may differ from the reference program's by a relative error of at most 0.0003.
Values sent between devices are 32-bit elements; how exact they have to be, the bound alone decides.
A program may use at most 64 MiB of HBM per device.

```python
import math
import jax
import jax.numpy as jnp
import numpy as np
from jax import lax

G = 128
TILES = 16
TILE = 128
NBR = 16
ITERS = 4
ATOMS_DEV = 2048
XDEV = 64
CELLS_DEV = 8192
LINES_DEV = 64
NLINES = 256
CAP = 8
N_PEN = 4


def draw_live_tiles(key, part):
    key = jax.random.fold_in(key, 7)
    key_counts, key_full, key_least = jax.random.split(key, 3)
    total = XDEV * N_PEN
    counts = jax.random.randint(key_counts, (total,), 1, TILES + 1)
    full_pick = jax.random.randint(key_full, (), 0, total)
    least_pick = (full_pick + 1 + jax.random.randint(key_least, (), 0, total - 1)) % total
    positions = jnp.arange(total)
    counts = jnp.where(positions == full_pick, TILES, counts)
    counts = jnp.where(positions == least_pick, 1, counts)
    return counts.reshape(XDEV, N_PEN).astype(jnp.int32)


def plant(drawn, own_key, low, high):
    longest = drawn.shape.index(max(drawn.shape))
    spots = []
    for shift in (0, 1):
        where = [jax.random.randint(jax.random.fold_in(own_key, axis), (), 0, length) for axis, length in enumerate(drawn.shape)]
        where[longest] = (where[longest] + shift) % drawn.shape[longest]
        spots.append(tuple(where))
    return drawn.at[spots[0]].set(low).at[spots[1]].set(high)


def block_scale(key, extent, shards, low, largest):
    level = 1.0
    for position, parts in shards:
        draws = jax.random.uniform(jax.random.fold_in(jax.random.fold_in(key, 6), position), (parts,), jnp.float32, low / len(shards), largest / len(shards))
        level = level * jnp.repeat(jnp.exp(draws), extent[position] // parts).reshape((-1,) + (1,) * (len(extent) - 1 - position))
    return level


def routed_block(own_key, own, number, rows, number_of, top, limit, lean):
    order = jax.random.permutation(own_key, number_of)
    crowded, usual = load_shares(number_of, rows * top, limit, lean, True), load_shares(number_of, rows * top, limit, lean, False)
    places = jnp.arange(number_of)

    def named(sizes, turn):
        used = int((sizes > 0).sum())
        fixed = max(1, used // 4)
        moved = fixed + (places - fixed + turn * (used - fixed)) % max(1, number_of - fixed)
        return jnp.zeros((number_of,), jnp.int32).at[order[jnp.where(places < fixed, places, moved)]].set(jnp.asarray(sizes, jnp.int32))

    sizes = jnp.where(number % 4 == 0, named(crowded, number // 4), named(usual, number - number // 4 - 1))
    mixed = jax.random.permutation(jax.random.fold_in(own, 3), number_of)
    giver, receiver = mixed[0:number_of // 2 * 2:2], mixed[1:number_of // 2 * 2:2]
    margin = jnp.minimum(sizes[giver] - 1, limit - sizes[receiver]) // 2
    margin = jnp.where((giver == order[0]) | (receiver == order[0]) | (sizes[receiver] == 0), 0, jnp.maximum(margin, 0))
    moved = jax.random.randint(jax.random.fold_in(own, 4), (number_of // 2,), 0, 1 << 20) % (margin + 1)
    sizes = sizes.at[giver].add(-moved).at[receiver].add(moved)
    members = jnp.searchsorted(jnp.cumsum(sizes), jnp.arange(rows * top), side="right").astype(jnp.int32)
    grid = members.reshape(top, rows).T
    grid = grid[jax.random.permutation(jax.random.fold_in(own, 1), rows)]
    turn = jax.random.randint(jax.random.fold_in(own, 2), (rows, 1), 0, top)
    return jnp.take_along_axis(grid, (jnp.arange(top)[None, :] + turn) % top, axis=1)


def load_shares(amount, total, most, lean, full):
    weights = [(1 << 20) // math.isqrt(grade ** lean) + 1 for grade in range(1, amount + 1)]
    largest = most if full else min(most, max(-(-total // amount), total * weights[0] // sum(weights)))
    least = 1 if total - largest >= amount - 1 else 0
    given, spare = [largest] + [least] * (amount - 1), total - largest - least * (amount - 1)
    while spare > 0:
        movable = [i for i in range(1, amount) if given[i] < largest] or [i for i in range(1, amount) if given[i] < most]
        pool, budget = sum([weights[i] for i in movable]), spare
        for i in movable:
            extra = min(most - given[i], max(1, budget * weights[i] // pool), spare)
            given[i] = given[i] + extra
            spare = spare - extra
    return np.array(given)


def gaussian(own_key, extent, width, reach, shards=(), kind=jnp.bfloat16):
    loudness = block_scale(own_key, extent, shards, -0.22, 0.18) if shards else 1.0
    array = jax.random.normal(own_key, extent, jnp.float32) * width * loudness
    return jnp.minimum(jnp.maximum(array, -reach), reach).astype(kind)


def setup_inputs(seed: int = 0) -> dict:
    keys = jax.random.split(jax.random.key(seed), 13)
    atom_positions = jnp.clip(1.0 * jax.random.uniform(keys[0], (XDEV, N_PEN, 3, ATOMS_DEV), jnp.float32) ** block_scale(keys[0], (XDEV, N_PEN, 3, ATOMS_DEV), ((0, 64), (1, 4)), -0.2, 0.2), 0.0, 1.0)
    atom_charges = gaussian(keys[1], (XDEV, N_PEN, ATOMS_DEV), 0.2, 1.2, ((0, 64), (1, 4)), jnp.float32)
    multipole_basis = gaussian(keys[2], (XDEV, N_PEN, 4, ATOMS_DEV), 1.0, 6.0, ((0, 64), (1, 4)), jnp.float32)
    spread_cell = plant(jax.random.randint(keys[3], (XDEV, N_PEN, 8, ATOMS_DEV), 0, NLINES * G), jax.random.fold_in(keys[3], 1), 0, (NLINES * G) - 1).astype(jnp.int32)
    spread_weight = jnp.clip(0.25 * jax.random.uniform(keys[4], (XDEV, N_PEN, 8, ATOMS_DEV), jnp.float32) ** block_scale(keys[4], (XDEV, N_PEN, 8, ATOMS_DEV), ((0, 64), (1, 4)), -0.2, 0.2), 0.0, 0.25)
    line_slab_keys = jax.random.split(jax.random.fold_in(keys[5], 1), XDEV * N_PEN * NLINES // NLINES)
    line_slab_turns = jax.random.permutation(jax.random.fold_in(keys[5], 3), XDEV * N_PEN * NLINES // NLINES)
    line_slab = jax.vmap(lambda own, number: routed_block(jax.random.fold_in(keys[5], 2), own, number, NLINES, XDEV, 1, CAP, 2))(line_slab_keys, line_slab_turns).reshape((XDEV, N_PEN, NLINES, 1))
    line_target = plant(jax.random.randint(keys[6], (XDEV, N_PEN, NLINES), 0, LINES_DEV), jax.random.fold_in(keys[6], 1), 0, LINES_DEV - 1).astype(jnp.int32)
    neighbour_tiles = plant(jax.random.randint(keys[7], (XDEV, N_PEN, TILES, NBR), 0, 9 * TILES), jax.random.fold_in(keys[7], 1), 0, (9 * TILES) - 1).astype(jnp.int32)
    live_tiles = draw_live_tiles(jax.random.fold_in(keys[12], 71), 0)
    initial_density = gaussian(keys[9], (G, G, G), 0.5, 3.0, ((0, 64), (1, 4)), jnp.float32)
    susceptibility = jnp.clip(jnp.exp(math.log(0.5) - 2.3025851 * jax.random.uniform(keys[10], (G, G, G), jnp.float32) ** block_scale(keys[10], (G, G, G), ((0, 64), (1, 4)), -0.2, 0.2)), 0.05, 0.5)
    ion_potential = gaussian(keys[11], (G, G, G), 1.0, 6.0, ((0, 64), (1, 4)), jnp.float32)
    return {"atom_positions": atom_positions, "atom_charges": atom_charges, "multipole_basis": multipole_basis, "spread_cell": spread_cell, "spread_weight": spread_weight, "line_slab": line_slab, "line_target": line_target, "neighbour_tiles": neighbour_tiles, "live_tiles": live_tiles, "initial_density": initial_density, "susceptibility": susceptibility, "ion_potential": ion_potential}


MIX_RATE = 0.3
SCREENING = 0.1
EWALD_BETA = 2.0
SOFTENING = 0.01
BOX_HEIGHT = 4.0

def to_blocks(grid_field):
    row_width = G // XDEV
    column_width = G // N_PEN
    shaped = grid_field.reshape(XDEV, row_width, N_PEN, column_width, G)
    return shaped.transpose(0, 2, 1, 3, 4).reshape(XDEV, N_PEN, row_width * column_width * G)

def from_blocks(blocks):
    row_width = G // XDEV
    column_width = G // N_PEN
    shaped = blocks.reshape(XDEV, N_PEN, row_width, column_width, G)
    return shaped.transpose(0, 2, 1, 3, 4).reshape(G, G, G)

def solve_field(grid_field):
    spectrum = jnp.fft.fftn(grid_field)
    frequency = jnp.arange(G)
    single = 2.0 - 2.0 * jnp.cos(2.0 * math.pi / G * frequency.astype(jnp.float32))
    eigen_sum = single[:, None, None] + single[None, :, None] + single[None, None, :]
    return jnp.real(jnp.fft.ifftn(spectrum / (SCREENING + eigen_sum))).astype(jnp.float32)

def tile_block(own_tiles, flat_halo, neighbour_ids, first_tile, tile_count, tiles_per_step):
    chosen = lax.dynamic_slice_in_dim(neighbour_ids, first_tile, tiles_per_step, 0)
    source_tile = chosen // tile_count
    local_tile = chosen % tile_count
    partner = flat_halo[source_tile, :, local_tile]
    offset_x = (source_tile // 3 - 1).astype(jnp.float32)[:, :, None]
    offset_y = (source_tile % 3 - 1).astype(jnp.float32)[:, :, None]
    own_block = lax.dynamic_slice_in_dim(own_tiles, first_tile, tiles_per_step, 1)
    delta_x = own_block[0][:, :, None, None] - (partner[:, :, 0] + offset_x)[:, None]
    delta_y = own_block[1][:, :, None, None] - (partner[:, :, 1] + offset_y)[:, None]
    delta_z = BOX_HEIGHT * (own_block[2][:, :, None, None] - partner[:, :, 2][:, None])
    distance = jnp.sqrt(delta_x * delta_x + delta_y * delta_y + delta_z * delta_z + SOFTENING)
    kernel = jax.scipy.special.erfc(EWALD_BETA * distance) / distance
    return lax.optimization_barrier(jnp.sum(partner[:, :, 3][:, None] * kernel, axis=(2, 3)))

def short_range(own_atoms, beside_all, neighbour_ids):
    tile_count = own_atoms.shape[1] // TILE
    flat_halo = beside_all.reshape(9, 4, tile_count, TILE)
    own_tiles = own_atoms.reshape(4, tile_count, TILE)
    tiles_per_step = 4
    starts = jnp.arange(tile_count // tiles_per_step, dtype=jnp.int32) * tiles_per_step

    def one_step(first_tile):
        return tile_block(own_tiles, flat_halo, neighbour_ids, first_tile, tile_count, tiles_per_step)
    return lax.map(one_step, starts).reshape(-1)

def reference(atom_positions, atom_charges, multipole_basis, spread_cell, spread_weight, line_slab, line_target, neighbour_tiles, live_tiles, initial_density, susceptibility, ion_potential):
    slot_tile = jnp.arange(ATOMS_DEV, dtype=jnp.int32) // TILE
    live_mask = (slot_tile[None, None, :] < live_tiles[:, :, None]).astype(jnp.float32)
    charge = atom_charges * live_mask

    def spread_one(cells, weights, charges):
        return jax.ops.segment_sum((weights * charges[None, :]).reshape(-1), cells.reshape(-1), num_segments=NLINES * G)
    charge_lines = jax.vmap(jax.vmap(spread_one))(spread_cell, spread_weight, charge).reshape(XDEV * N_PEN * NLINES, G)
    column = jnp.arange(N_PEN, dtype=jnp.int32)[None, :, None]
    global_line = ((line_slab[:, :, :, 0] * N_PEN + column) * LINES_DEV + line_target).astype(jnp.int32).reshape(-1)
    grid_lines = jax.ops.segment_sum(charge_lines, global_line, num_segments=XDEV * N_PEN * LINES_DEV)
    mm_grid = from_blocks(grid_lines.reshape(XDEV, N_PEN, CELLS_DEV))
    rho = initial_density
    potential = jnp.zeros_like(rho)
    for iteration in range(ITERS):
        potential = solve_field(rho + mm_grid)
        rho = rho - MIX_RATE * (rho + susceptibility * (potential + ion_potential))
    density = rho
    coords = 1.0 + 2.0 * (jnp.arange(G).astype(jnp.float32) + 0.5) / G
    coord_x = coords[:, None, None]
    coord_y = coords[None, :, None]
    coord_z = coords[None, None, :]
    moments = jnp.stack([jnp.sum(density * coord_x), jnp.sum(density * coord_y), jnp.sum(density * coord_x * coord_y), jnp.sum(density * coord_z)])
    moments = moments * (1.0 / (G * math.sqrt(G)))
    packed = jnp.concatenate([atom_positions, charge[:, :, None, :]], axis=2)
    padded = jnp.pad(packed, ((1, 1), (1, 1), (0, 0), (0, 0)))

    def per_domain(flat_index):
        row = (flat_index // N_PEN).astype(jnp.int32)
        col = (flat_index % N_PEN).astype(jnp.int32)
        zero = jnp.zeros((), jnp.int32)
        beside_all = lax.dynamic_slice(padded, (row, col, zero, zero), (3, 3, 4, ATOMS_DEV))
        own_atoms = lax.dynamic_slice(packed, (row, col, zero, zero), (1, 1, 4, ATOMS_DEV))[0, 0]
        neighbour_ids = lax.dynamic_slice(neighbour_tiles, (row, col, zero, zero), (1, 1, TILES, NBR))[0, 0]
        return short_range(own_atoms, beside_all, neighbour_ids)
    short_all = lax.map(per_domain, jnp.arange(XDEV * N_PEN, dtype=jnp.int32)).reshape(XDEV, N_PEN, ATOMS_DEV)
    potential_lines = to_blocks(potential).reshape(XDEV * N_PEN * LINES_DEV, G)
    line_potential = jnp.take(potential_lines, global_line, axis=0).reshape(XDEV, N_PEN, NLINES * G)

    def interpolate(line_values, cells, weights):
        return lax.optimization_barrier(jnp.sum(weights * jnp.take(line_values, cells, axis=0), axis=0))
    long_range = jax.vmap(jax.vmap(interpolate))(line_potential, spread_cell, spread_weight)
    far_field = lax.optimization_barrier(jnp.sum(moments[None, None, :, None] * multipole_basis, axis=2))
    mm_potential = live_mask * (short_all + long_range + far_field)
    return (potential, density, mm_potential)
```

```python
import functools
import math

import jax
import jax.numpy as jnp
import ml_dtypes
import numpy as np
from jax import lax
from jax.experimental import pallas as pl
from jax.experimental.pallas import tpu as pltpu
from jax.sharding import PartitionSpec as P

MESH = pl.DeviceIdType.MESH
F32 = jnp.float32
BF16 = jnp.bfloat16
G = 128
TILE = 128
TILES = 16
NBR = 16
ITERS = 4
ROWS = 64
PEN = 4
CAP = 8
NLINES = 256
MIX_RATE = 0.3
SCREENING = 0.1
BOX_HEIGHT = 4.0
SOFTENING = 0.01
ERF_SHIFT = 1.35
ERF_POLY = (
    8.048848463632075e-05,
    0.279831566396696,
    0.40782855654035,
    0.3006583844815809,
    1.260144403309312,
    -1.158323294058104,
    2.9062706842895354,
    -1.262709002135607,
)
VMEM_LIMIT = 48 * 1024 * 1024


def halves(table):
    high = table.astype(ml_dtypes.bfloat16)
    low = (table - high.astype(np.float64)).astype(ml_dtypes.bfloat16)
    return [high, low]


def tables():
    k = np.arange(G)
    angle = 2.0 * np.pi * (np.outer(k, k) % G) / G
    cas = (np.cos(angle) + np.sin(angle)) / np.sqrt(G)
    order = np.concatenate([np.arange(32) + 32 * (2 * z + c) for c in range(2) for z in range(2)])
    split_x = np.concatenate([np.arange(ROWS) * 2, np.arange(ROWS) * 2 + 1])
    square = halves(cas) + halves(cas[:, order]) + halves(cas[:, split_x]) + halves(cas[split_x, :])
    wide = np.zeros((2, G, 2, 2, ROWS))
    for x in range(2):
        for h in range(2):
            wide[x, :, h, x, :] = cas[:, h * ROWS : (h + 1) * ROWS]
    wide = wide.reshape(2 * G, 2 * G)
    big = halves(wide) + halves(wide.T)
    lam = 2.0 - 2.0 * np.cos(2.0 * np.pi * k / G)
    lam_rows = np.repeat(lam[:, None], G, axis=1)
    lam_lanes = np.zeros((8, G))
    for h in range(2):
        lam_lanes[h] = np.tile(lam[h * ROWS : (h + 1) * ROWS], 2)
    flat = np.concatenate([lam_rows, lam_lanes]).astype(np.float32)
    return np.stack(square), np.stack(big), flat


def split(x):
    high = x.astype(BF16)
    return high, (x - high.astype(F32)).astype(BF16)


def dot(a, b):
    return jnp.dot(a, b, preferred_element_type=F32)


def dot_nt(a, b):
    return lax.dot_general(a, b, (((1,), (1,)), ((), ())), preferred_element_type=F32)


def dot_tn(a, b):
    return lax.dot_general(a, b, (((0,), (0,)), ((), ())), preferred_element_type=F32)


def left_const(high, low, x):
    x_high, x_low = split(x)
    return dot(high, x_high) + (dot(high, x_low) + dot(low, x_high))


def right_const(x, high, low):
    x_high, x_low = split(x)
    return dot(x_high, high) + (dot(x_low, high) + dot(x_high, low))


def iota(shape, dim):
    return lax.broadcasted_iota(jnp.int32, shape, dim)


CHUNK = 512


def spread_kernel(
    live_ref, cell_ref, weight_ref, charge_row_ref, positions_ref, charge_ref,
    slab_col_ref, slab_row_ref, target_row_ref, send_ref, packed_ref, slot_ref,
):
    live = live_ref[0, 0]
    tile_of = iota((TILES, TILE), 0)
    for axis in range(3):
        packed_ref[axis * TILES : (axis + 1) * TILES, :] = positions_ref[axis]
    packed_ref[3 * TILES : 4 * TILES, :] = jnp.where(tile_of < live, charge_ref[...], 0.0)
    packed_ref[4 * TILES : 4 * TILES + 8, :] = jnp.zeros((8, TILE), F32) + live.astype(F32)

    slab_row = slab_row_ref[...]
    same = (slab_col_ref[...] == slab_row) & (iota((NLINES, NLINES), 0) < iota((NLINES, NLINES), 1))
    rank = jnp.sum(same.astype(F32), axis=0, keepdims=True).astype(jnp.int32)
    slot = slab_row * CAP + rank
    slot_ref[...] = slot
    pick = (iota((ROWS * CAP, NLINES), 0) == slot).astype(F32).astype(BF16)
    owner = jnp.where(iota((ROWS, NLINES), 0) == slab_row, target_row_ref[...].astype(F32), 0.0)
    place = (iota((TILE, NLINES), 0) == rank).astype(F32)
    targets = dot_nt(owner.astype(BF16), place.astype(BF16))

    line_iota = iota((NLINES, CHUNK), 0)
    cell_iota = iota((G, CHUNK), 0)

    def step(chunk, total):
        where = pl.ds(pl.multiple_of(chunk * CHUNK, CHUNK), CHUNK)
        atom = chunk * CHUNK + iota((1, CHUNK), 1)
        charge = jnp.where(atom // TILE < live, charge_row_ref[:, where], 0.0)
        for corner in range(8):
            cell = cell_ref[corner : corner + 1, where]
            high, low = split(weight_ref[corner : corner + 1, where] * charge)
            hit = line_iota == cell // G
            lines = jnp.concatenate(
                [
                    jnp.where(hit, high.astype(F32), 0.0).astype(BF16),
                    jnp.where(hit, low.astype(F32), 0.0).astype(BF16),
                ],
                axis=0,
            )
            spots = (cell_iota == cell % G).astype(F32).astype(BF16)
            total = total + dot_nt(lines, spots)
        return total

    total = lax.fori_loop(
        0, TILES * TILE // CHUNK, step, jnp.zeros((2 * NLINES, G), F32)
    )
    lines_high, lines_low = split(total[:NLINES] + total[NLINES:])
    send_ref[:, :CAP, :] = (dot(pick, lines_high) + dot(pick, lines_low)).reshape(ROWS, CAP, G)
    send_ref[:, CAP, :] = targets
    send_ref[:, CAP + 1 :, :] = jnp.zeros((ROWS, 16 - CAP - 1, G), F32)


def field_kernel(
    send_ref, packed_ref, rho_ref, sus_ref, ion_ref, square_ref, big_ref, flat_ref,
    pot_out, rho_out, halo_ref, back_ref,
    line_buf, mm, rho, sus, ion, fwd_send, fwd_recv, ret_send, ret_recv, green, line_send, last_pot,
    line_sems, pen_sems, mm_sems, halo_send_sems, halo_recv_sems, fwd_sems, ret_sems, core_sems, back_sems,
):
    group, dom, pen = lax.axis_index("group"), lax.axis_index("dom"), lax.axis_index("pen")
    me = group * 16 + dom
    core, z_lo = lax.rem(pen, 2), pen // 2
    other_chip = lax.rem(pen + 2, PEN)
    sibling = z_lo * 2 + (1 - core)

    def device(row, column):
        return (row // 16, lax.rem(row, 16), column)

    def remote(src, dst, send_sem, recv_sem, row, column):
        return pltpu.make_async_remote_copy(
            src_ref=src, dst_ref=dst, send_sem=send_sem, recv_sem=recv_sem,
            device_id=device(row, column), device_id_type=MESH,
        )

    barrier = pltpu.get_barrier_semaphore()

    def greet(k, carry):
        row = lax.rem(me + k, ROWS)
        pl.semaphore_signal(barrier, inc=1, device_id=device(row, pen), device_id_type=MESH)
        pl.semaphore_signal(barrier, inc=1, device_id=device(row, other_chip), device_id_type=MESH)
        return carry

    lax.fori_loop(1, ROWS, greet, 0)
    for k in (1, 2, 3):
        pl.semaphore_signal(
            barrier, inc=1, device_id=device(me, lax.rem(pen + k, PEN)), device_id_type=MESH
        )
    for dx in (1, ROWS - 1):
        for dy in (1, PEN - 1):
            pl.semaphore_signal(
                barrier, inc=1, device_id=device(lax.rem(me + dx, ROWS), lax.rem(pen + dy, PEN)),
                device_id_type=MESH,
            )
    pl.semaphore_wait(barrier, 2 * (ROWS - 1) + 3 + 4)

    def send_lines(k, carry):
        row = lax.rem(me + k, ROWS)
        remote(
            send_ref.at[row, pl.ds(0, CAP + 1)], line_buf.at[me, pl.ds(0, CAP + 1)],
            line_sems.at[0], line_sems.at[1], row, pen,
        ).start()
        return carry

    lax.fori_loop(1, ROWS, send_lines, 0)
    line_buf[me] = send_ref[me]

    columns = pl.ds(pl.multiple_of(pen * 32, 32), 32)
    slabs = ((rho_ref, rho), (sus_ref, sus), (ion_ref, ion))

    def slab_copy(index, k):
        source, whole = slabs[index]
        return remote(
            source, whole.at[:, columns, :],
            pen_sems.at[0, index, k - 1], pen_sems.at[1, index, k - 1],
            me, lax.rem(pen + k, PEN),
        )

    for index in range(3):
        for k in (1, 2, 3):
            slab_copy(index, k).start()

    neighbours = [(dx, dy) for dx in (-1, 0, 1) for dy in (-1, 0, 1) if (dx, dy) != (0, 0)]

    def halo_copy(dx, dy):
        number = (1 - dx) * 3 + 1 - dy
        return remote(
            packed_ref, halo_ref.at[number], halo_send_sems.at[number], halo_recv_sems.at[number],
            lax.rem(me + dx + ROWS, ROWS), lax.rem(pen + dy + PEN, PEN),
        )

    for dx, dy in neighbours:
        halo_copy(dx, dy).start()

    halo_ref[4] = packed_ref[...]
    for source, whole in slabs:
        whole[:, columns, :] = source[...]

    lane = iota((G, G), 1)
    half = me // 32
    y_row = pen * 32 + lax.rem(me, 32)
    lam_yz = flat_ref[pl.ds(y_row, 1), :] + flat_ref[pl.ds(G + half, 1), :]
    green[...] = 1.0 / (SCREENING + (flat_ref[0:G, :] + lam_yz))

    def whole_line_copy(ref, sems):
        return pltpu.make_async_remote_copy(
            src_ref=ref.at[pl.ds(0, ROWS - 1), pl.ds(0, CAP + 1)],
            dst_ref=ref.at[pl.ds(0, ROWS - 1), pl.ds(0, CAP + 1)],
            send_sem=sems.at[0], recv_sem=sems.at[1],
            device_id=device(lax.rem(me + 1, ROWS), pen), device_id_type=MESH,
        )

    whole_line_copy(line_buf, line_sems).wait_recv()
    source_of = iota((ROWS * CAP, ROWS), 0) // CAP == iota((ROWS * CAP, ROWS), 1)
    spread_targets = dot(source_of.astype(F32).astype(BF16), line_buf[:, CAP, :].astype(BF16))
    own_lane = iota((ROWS * CAP, G), 1) == lax.rem(iota((ROWS * CAP, G), 0), CAP)
    target = jnp.sum(jnp.where(own_lane, spread_targets, 0.0), axis=1, keepdims=True)
    landing = (target == iota((ROWS * CAP, ROWS), 1).astype(F32)).astype(F32)
    landing_t = landing.T.astype(BF16)
    landing = landing.astype(BF16)
    lines_high, lines_low = split(line_buf[:, :CAP, :].reshape(ROWS * CAP, G))
    own_mm = dot(landing_t, lines_high) + dot(landing_t, lines_low)
    for x in range(2):
        mm[x, columns, :] = own_mm[x * 32 : (x + 1) * 32]

    def mm_copy(k):
        return remote(
            mm.at[:, columns, :], mm.at[:, columns, :], mm_sems.at[0, k - 1], mm_sems.at[1, k - 1],
            me, lax.rem(pen + k, PEN),
        )

    for k in (1, 2, 3):
        mm_copy(k).start()
    for index in range(3):
        for k in (1, 2, 3):
            slab_copy(index, k).wait_recv()
    for k in (1, 2, 3):
        mm_copy(k).wait_recv()

    low_lanes = iota((ROWS, G), 1) < ROWS
    chunk_rows = pl.ds(pl.multiple_of(pen * 32, 32), 32)

    def fwd_all():
        return pltpu.make_async_remote_copy(
            src_ref=fwd_send.at[pl.ds(0, ROWS - 1)], dst_ref=fwd_recv.at[pl.ds(0, ROWS - 1)],
            send_sem=fwd_sems.at[0], recv_sem=fwd_sems.at[1],
            device_id=device(lax.rem(me + 1, ROWS), pen), device_id_type=MESH,
        )

    def ret_copy(slot, row, column):
        return remote(
            ret_send.at[pl.ds(row, 1)],
            ret_recv.at[slot, half, core, z_lo, pl.ds(lax.rem(me, 32), 1)],
            ret_sems.at[0], ret_sems.at[1 + slot], row, column,
        )

    def ret_all(slot):
        most = ret_send.at[pl.ds(0, 2 * ROWS - 1)]
        return pltpu.make_async_remote_copy(
            src_ref=most, dst_ref=most,
            send_sem=ret_sems.at[0], recv_sem=ret_sems.at[1 + slot],
            device_id=device(lax.rem(me + 1, ROWS), pen), device_id_type=MESH,
        )

    def core_copy(slot, h):
        return remote(
            ret_recv.at[slot, h, core], ret_recv.at[slot, h, core],
            core_sems.at[0, slot, h], core_sems.at[1, slot, h], me, sibling,
        )

    for iteration in range(ITERS):
        slot = iteration % 2
        source = jnp.concatenate([rho[0] + mm[0], rho[1] + mm[1]], axis=1)
        spectrum = left_const(square_ref[0, chunk_rows, :], square_ref[1, chunk_rows, :], source)
        spectrum = right_const(spectrum, big_ref[0], big_ref[1])
        if iteration > 0:
            fwd_all().wait_send()
        fwd_send[0:32, :] = spectrum[:, :G]
        fwd_send[32:64, :] = spectrum[:, G:]

        def send_fwd(k, carry):
            row = lax.rem(me + k, ROWS)
            remote(
                fwd_send.at[pl.ds(row, 1)], fwd_recv.at[pl.ds(me, 1)],
                fwd_sems.at[0], fwd_sems.at[1], row, pen,
            ).start()
            return carry

        lax.fori_loop(1, ROWS, send_fwd, 0)
        fwd_recv[pl.ds(me, 1), :] = fwd_send[pl.ds(me, 1), :]
        fwd_all().wait_recv()
        received = fwd_recv[...]
        both = jnp.concatenate([received, pltpu.roll(received, ROWS, 1)], axis=0)
        modes = left_const(square_ref[4], square_ref[5], both) * green[...]
        solved = left_const(square_ref[6], square_ref[7], modes)
        if iteration > 0:
            ret_all(1 - slot).wait_send()
        ret_send[:ROWS, :] = jnp.where(low_lanes, solved[:ROWS], pltpu.roll(solved[ROWS:], ROWS, 1))

        def send_ret(k, carry):
            row = lax.rem(me + k, ROWS)
            ret_copy(slot, row, pen).start()
            ret_copy(slot, row, other_chip).start()
            return carry

        lax.fori_loop(1, ROWS, send_ret, 0)
        ret_copy(slot, me, other_chip).start()
        ret_recv[slot, half, core, z_lo, pl.ds(lax.rem(me, 32), 1)] = ret_send[pl.ds(me, 1), :]
        ret_all(slot).wait_recv()
        for h in range(2):
            core_copy(slot, h).start()
        for h in range(2):
            core_copy(slot, h).wait_recv()
        lines = jnp.concatenate([ret_recv[slot, h].reshape(G, G) for h in range(2)], axis=1)
        lines = right_const(lines, big_ref[2], big_ref[3])
        potential = left_const(square_ref[2], square_ref[3], lines)
        for x in range(2):
            own = potential[:, x * G : (x + 1) * G]
            if iteration == ITERS - 1:
                last_pot[x] = own
            rho[x] = rho[x] - MIX_RATE * (rho[x] + sus[x] * (own + ion[x]))
        for h in range(2):
            core_copy(slot, h).wait_send()

    row_u = 1.0 + 2.0 * (iota((G, G), 0).astype(F32) + 0.5) / G
    lane_u = 1.0 + 2.0 * (lane.astype(F32) + 0.5) / G
    x_u = [1.0 + 2.0 * ((2 * me + x).astype(F32) + 0.5) / G for x in range(2)]
    weighted = rho[0] * x_u[0] + rho[1] * x_u[1]
    plain = rho[0] + rho[1]
    sums = [weighted, plain * row_u, weighted * row_u, plain * lane_u]
    own_moments = jnp.zeros((1, G), F32)
    for index, term in enumerate(sums):
        value = jnp.sum(jnp.sum(term, axis=0, keepdims=True), axis=1, keepdims=True)
        own_moments = jnp.where(iota((1, G), 1) == index, value, own_moments)
    own_pot = jnp.concatenate([last_pot[x, columns, :] for x in range(2)], axis=0)
    pot_high, pot_low = split(own_pot)
    line_send[:, :CAP, :] = (dot(landing, pot_high) + dot(landing, pot_low)).reshape(ROWS, CAP, G)
    line_send[:, CAP, :] = jnp.broadcast_to(own_moments, (ROWS, G))

    def send_back(k, carry):
        row = lax.rem(me + k, ROWS)
        remote(
            line_send.at[row, pl.ds(0, CAP + 1)], back_ref.at[me, pl.ds(0, CAP + 1)],
            back_sems.at[0], back_sems.at[1], row, pen,
        ).start()
        return carry

    lax.fori_loop(1, ROWS, send_back, 0)
    back_ref[me, 0 : CAP + 1, :] = line_send[me, 0 : CAP + 1, :]
    for x in range(2):
        pot_out[x] = last_pot[x, columns, :]
        rho_out[x] = rho[x, columns, :]

    last = (ITERS - 1) % 2
    for dx, dy in neighbours:
        halo_copy(dx, dy).wait()
    for dx, dy in neighbours:
        outside = (me + dx < 0) | (me + dx >= ROWS) | (pen + dy < 0) | (pen + dy >= PEN)

        @pl.when(outside)
        def _():
            halo_ref[(dx + 1) * 3 + dy + 1] = jnp.zeros_like(packed_ref)

    whole_line_copy(line_buf, line_sems).wait_send()
    for k in (1, 2, 3):
        for index in range(3):
            slab_copy(index, k).wait_send()
        mm_copy(k).wait_send()
    fwd_all().wait_send()
    ret_all(last).wait_send()
    whole_line_copy(line_send, back_sems).wait()


def pair_values(own, partner, rows):
    x, y, z = own
    dx = x - partner[0]
    dy = y - partner[1]
    dz = z - partner[2]
    s = dx * dx + dy * dy + dz * dz + SOFTENING
    u = lax.rsqrt(s)
    t = 1.0 / (s * u + ERF_SHIFT)
    poly = jnp.full_like(t, ERF_POLY[-1])
    for coefficient in ERF_POLY[-2::-1]:
        poly = poly * t + coefficient
    return (partner[3] * u) * (poly * jnp.exp(-4.0 * s))


def atom_kernel(
    live_ref, nbr_ref, halo_ref, back_ref, slot_ref, cell_ref, weight_ref, basis_ref, out_ref,
    columns, acc, short,
):
    live = live_ref[0, 0]
    for axis in range(3):
        columns[axis] = halo_ref[4, axis * TILES : (axis + 1) * TILES, :].T * (
            BOX_HEIGHT if axis == 2 else 1.0
        )
    live_of = [jnp.max(halo_ref[d, 4 * TILES : 4 * TILES + 1, :]) for d in range(9)]
    tile_lane = iota((TILE, TILES), 1)

    def own_tile(t, carry):
        own = [
            jnp.sum(jnp.where(tile_lane == t, columns[axis], 0.0), axis=1, keepdims=True)
            for axis in range(3)
        ]
        own = [jnp.broadcast_to(c, (TILE, TILE)) for c in own]
        acc[...] = jnp.zeros_like(acc)

        def partner_tile(n, carry):
            chosen = nbr_ref[t, n]
            d = chosen // TILES
            tile = lax.rem(chosen, TILES)
            there = live_of[0]
            for index in range(1, 9):
                there = jnp.where(d == index, live_of[index], there)

            @pl.when(tile.astype(F32) < there)
            def _():
                row = [halo_ref[d, pl.ds(axis * TILES + tile, 1), :] for axis in range(4)]
                row[0] = row[0] + (d // 3 - 1).astype(F32)
                row[1] = row[1] + (lax.rem(d, 3) - 1).astype(F32)
                row[2] = row[2] * BOX_HEIGHT
                for part in range(4):
                    rows = slice(part * 32, part * 32 + 32)
                    acc[rows, :] += pair_values([c[rows, :] for c in own], row, rows)

            return carry

        lax.fori_loop(0, NBR, partner_tile, 0)
        short[:, pl.ds(pl.multiple_of(t * TILE, TILE), TILE)] = jnp.sum(
            acc[...].T, axis=0, keepdims=True
        )
        return carry

    lax.fori_loop(0, live, own_tile, 0)

    slot = slot_ref[...]
    pick = (iota((ROWS * CAP, NLINES), 0) == slot).astype(F32).astype(BF16)
    back_high, back_low = split(back_ref[:, :CAP, :].reshape(ROWS * CAP, G))
    values = dot_tn(jnp.concatenate([back_high, back_low], axis=1), pick)
    values_high, values_low = split(values[:G] + values[G:])
    values = jnp.concatenate([values_high, values_low], axis=0)
    moments = jnp.sum(back_ref[:, CAP, :], axis=0, keepdims=True) * (1.0 / (G * math.sqrt(G)))
    moment = [
        jnp.sum(jnp.where(iota((1, G), 1) == m, moments, 0.0), axis=1, keepdims=True)
        for m in range(4)
    ]
    line_iota = iota((NLINES, CHUNK), 0)
    cell_iota = iota((G, CHUNK), 0)

    def step(chunk, carry):
        where = pl.ds(pl.multiple_of(chunk * CHUNK, CHUNK), CHUNK)
        total = jnp.zeros((1, CHUNK), F32)
        for corner in range(8):
            cell = cell_ref[corner : corner + 1, where]
            lines = (line_iota == cell // G).astype(F32).astype(BF16)
            found = dot(values, lines)
            found = jnp.where(cell_iota == cell % G, found[:G] + found[G:], 0.0)
            total = total + weight_ref[corner : corner + 1, where] * jnp.sum(
                found, axis=0, keepdims=True
            )
        for m in range(4):
            total = total + moment[m] * basis_ref[m : m + 1, where]
        atom = chunk * CHUNK + iota((1, CHUNK), 1)
        out_ref[:, where] = jnp.where(atom // TILE < live, total + short[:, where], 0.0)
        return carry

    lax.fori_loop(0, TILES * TILE // CHUNK, step, 0)


def shards(
    atom_positions, atom_charges, multipole_basis, spread_cell, spread_weight, line_slab,
    line_target, neighbour_tiles, live_tiles, initial_density, susceptibility, ion_potential,
):
    vmem = pl.BlockSpec(memory_space=pltpu.VMEM)
    smem = pl.BlockSpec(memory_space=pltpu.SMEM)
    atoms = TILES * TILE
    cells = spread_cell[0, 0]
    weights = spread_weight[0, 0]
    packed_rows = 4 * TILES + 8
    send, packed, slot = pl.pallas_call(
        spread_kernel,
        out_shape=(
            jax.ShapeDtypeStruct((ROWS, 16, G), F32),
            jax.ShapeDtypeStruct((packed_rows, TILE), F32),
            jax.ShapeDtypeStruct((1, NLINES), jnp.int32),
        ),
        in_specs=[smem] + [vmem] * 8,
        out_specs=(vmem,) * 3,
        compiler_params=pltpu.CompilerParams(vmem_limit_bytes=VMEM_LIMIT),
        name="spread",
    )(
        live_tiles, cells, weights, atom_charges[0], atom_positions[0, 0].reshape(3, TILES, TILE),
        atom_charges.reshape(TILES, TILE), line_slab[0, 0], line_slab.reshape(1, NLINES),
        line_target[0],
    )
    square, big, flat = (jnp.asarray(table) for table in tables())
    block = initial_density.shape
    dma = pltpu.SemaphoreType.DMA
    potential, density, halo, back = pl.pallas_call(
        field_kernel,
        out_shape=(
            jax.ShapeDtypeStruct(block, F32),
            jax.ShapeDtypeStruct(block, F32),
            jax.ShapeDtypeStruct((9, packed_rows, TILE), F32),
            jax.ShapeDtypeStruct((ROWS, 16, G), F32),
        ),
        in_specs=[vmem] * 8,
        out_specs=(vmem,) * 4,
        scratch_shapes=[
            pltpu.VMEM((ROWS, 16, G), F32),
            pltpu.VMEM((2, G, G), F32),
            pltpu.VMEM((2, G, G), F32),
            pltpu.VMEM((2, G, G), F32),
            pltpu.VMEM((2, G, G), F32),
            pltpu.VMEM((ROWS, G), F32),
            pltpu.VMEM((ROWS, G), F32),
            pltpu.VMEM((2 * ROWS, G), F32),
            pltpu.VMEM((2, 2, 2, 2, 32, G), F32),
            pltpu.VMEM((G, G), F32),
            pltpu.VMEM((ROWS, 16, G), F32),
            pltpu.VMEM((2, G, G), F32),
            dma((2,)),
            dma((2, 3, 3)),
            dma((2, 3)),
            dma((9,)),
            dma((9,)),
            dma((2,)),
            dma((3,)),
            dma((2, 2, 2)),
            dma((2,)),
        ],
        compiler_params=pltpu.CompilerParams(
            collective_id=0, has_side_effects=True, vmem_limit_bytes=VMEM_LIMIT
        ),
        name="field",
    )(send, packed, initial_density, susceptibility, ion_potential, square, big, flat)
    values = pl.pallas_call(
        atom_kernel,
        out_shape=jax.ShapeDtypeStruct((1, atoms), F32),
        in_specs=[smem] * 2 + [vmem] * 6,
        out_specs=vmem,
        scratch_shapes=[
            pltpu.VMEM((3, TILE, TILES), F32),
            pltpu.VMEM((TILE, TILE), F32),
            pltpu.VMEM((1, atoms), F32),
        ],
        compiler_params=pltpu.CompilerParams(vmem_limit_bytes=VMEM_LIMIT),
        name="atoms",
    )(live_tiles, neighbour_tiles[0, 0], halo, back, slot, cells, weights, multipole_basis[0, 0])
    return potential, density, values[None]


def solution(mesh):
    row = ("group", "dom")
    placed = (
        P(row, "pen", None, None),
        P(row, "pen", None),
        P(row, "pen", None, None),
        P(row, "pen", None, None),
        P(row, "pen", None, None),
        P(row, "pen", None, None),
        P(row, "pen", None),
        P(row, "pen", None, None),
        P(row, "pen"),
        P(row, "pen", None),
        P(row, "pen", None),
        P(row, "pen", None),
    )
    return jax.shard_map(
        shards,
        mesh=mesh,
        in_specs=placed,
        out_specs=(P(row, "pen", None), P(row, "pen", None), P(row, "pen", None)),
        check_vma=False,
    )
```

```python
import math

import jax
import jax.numpy as jnp
import ml_dtypes
import numpy as np
from jax import lax
from jax.experimental import pallas as pl
from jax.experimental.pallas import tpu as pltpu
from jax.sharding import PartitionSpec as P

MESH = pl.DeviceIdType.MESH
F32 = jnp.float32
BF16 = jnp.bfloat16
G = 128
TILE = 128
TILES = 16
NBR = 16
ITERS = 4
ROWS = 64
PEN = 4
CAP = 8
NLINES = 256
MIX_RATE = 0.3
SCREENING = 0.1
BOX_HEIGHT = 4.0
SOFTENING = 0.01
ERF_SHIFT = 1.35
ERF_POLY = (
    8.048848463632075e-05,
    0.279831566396696,
    0.40782855654035,
    0.3006583844815809,
    1.260144403309312,
    -1.158323294058104,
    2.9062706842895354,
    -1.262709002135607,
)
VMEM_LIMIT = 64 * 1024 * 1024


def halves(table):
    high = table.astype(ml_dtypes.bfloat16)
    low = (table - high.astype(np.float64)).astype(ml_dtypes.bfloat16)
    return [high, low]


def tables():
    k = np.arange(G)
    angle = 2.0 * np.pi * (np.outer(k, k) % G) / G
    cas = (np.cos(angle) + np.sin(angle)) / np.sqrt(G)
    order = np.concatenate([np.arange(32) + 32 * (2 * z + c) for c in range(2) for z in range(2)])
    split_x = np.concatenate([np.arange(ROWS) * 2, np.arange(ROWS) * 2 + 1])
    square = halves(cas) + halves(cas[:, order]) + halves(cas[:, split_x]) + halves(cas[split_x, :])
    wide = np.zeros((2, G, 2, 2, ROWS))
    for x in range(2):
        for h in range(2):
            wide[x, :, h, x, :] = cas[:, h * ROWS : (h + 1) * ROWS]
    wide = wide.reshape(2 * G, 2 * G)
    big = halves(wide) + halves(wide.T)
    lam = 2.0 - 2.0 * np.cos(2.0 * np.pi * k / G)
    lam_rows = np.repeat(lam[:, None], G, axis=1)
    lam_lanes = np.zeros((8, G))
    for h in range(2):
        lam_lanes[h] = np.tile(lam[h * ROWS : (h + 1) * ROWS], 2)
    flat = np.concatenate([lam_rows, lam_lanes]).astype(np.float32)
    big = [part[:, h * G : (h + 1) * G] for part in big for h in range(2)]
    return np.stack(square), np.stack(big), flat


def split(x):
    high = x.astype(BF16)
    return high, (x - high.astype(F32)).astype(BF16)


def dot(a, b):
    return jnp.dot(a, b, preferred_element_type=F32)


def dot_nt(a, b):
    return lax.dot_general(a, b, (((1,), (1,)), ((), ())), preferred_element_type=F32)


def dot_tn(a, b):
    return lax.dot_general(a, b, (((0,), (0,)), ((), ())), preferred_element_type=F32)


def left_const(high, low, x):
    x_high, x_low = split(x)
    return dot(high, x_high) + (dot(high, x_low) + dot(low, x_high))


def right_const(x, high, low):
    x_high, x_low = split(x)
    return dot(x_high, high) + (dot(x_low, high) + dot(x_high, low))


def iota(shape, dim):
    return lax.broadcasted_iota(jnp.int32, shape, dim)


CHUNK = 512
FWD_TILES = 2
RET_TILES = 1


def pair_values(own, partner):
    dx = own[0] - partner[0]
    dy = own[1] - partner[1]
    dz = own[2] - partner[2]
    s = dx * dx + dy * dy + dz * dz + SOFTENING
    u = lax.rsqrt(s)
    t = 1.0 / (s * u + ERF_SHIFT)
    poly = jnp.full_like(t, ERF_POLY[-1])
    for coefficient in ERF_POLY[-2::-1]:
        poly = poly * t + coefficient
    return (partner[3] * u) * (poly * jnp.exp(-4.0 * s))


def kernel(
    live_ref, nbr_ref, cell_hbm, weight_hbm, positions_hbm, charge_hbm, slab_hbm, target_hbm,
    rho_hbm, sus_hbm, ion_hbm, basis_hbm, square_hbm, big_hbm, flat_hbm,
    pot_out, rho_out, mm_out,
    cells, weights, charges, slab_buf, target_buf, basis_ref, square_ref, big_ref, flat_ref,
    send_ref, line_buf, halo_ref, mm, rho, sus, ion, fwd_send, fwd_recv, ret_send, ret_recv,
    green, line_send, last_pot, back_ref, columns_of, short,
    load_sems, line_sems, pen_sems, mm_sems, halo_send_sems, halo_recv_sems, fwd_sems, ret_sems,
    core_sems, back_sems,
):
    group, dom, pen = lax.axis_index("group"), lax.axis_index("dom"), lax.axis_index("pen")
    me = group * 16 + dom
    core, z_lo = lax.rem(pen, 2), pen // 2
    other_chip = lax.rem(pen + 2, PEN)
    sibling = z_lo * 2 + (1 - core)
    columns = pl.ds(pl.multiple_of(pen * 32, 32), 32)
    live = live_ref[0, 0]

    first = [
        pltpu.make_async_copy(source, target, load_sems.at[index])
        for index, (source, target) in enumerate(
            (
                (cell_hbm, cells),
                (weight_hbm, weights),
                (charge_hbm, charges),
                (slab_hbm, slab_buf),
                (target_hbm, target_buf),
                (positions_hbm, halo_ref.at[4, pl.ds(0, 3 * TILES)]),
            )
        )
    ]
    later = [
        pltpu.make_async_copy(source, target, load_sems.at[6 + index])
        for index, (source, target) in enumerate(
            (
                (rho_hbm, rho.at[:, columns, :]),
                (sus_hbm, sus.at[:, columns, :]),
                (ion_hbm, ion.at[:, columns, :]),
                (flat_hbm, flat_ref),
                (square_hbm, square_ref),
                (big_hbm, big_ref),
                (basis_hbm, basis_ref),
            )
        )
    ]
    for copy in first + later:
        copy.start()

    def device(row, column):
        return (row // 16, lax.rem(row, 16), column)

    def remote(src, dst, send_sem, recv_sem, row, column):
        return pltpu.make_async_remote_copy(
            src_ref=src, dst_ref=dst, send_sem=send_sem, recv_sem=recv_sem,
            device_id=device(row, column), device_id_type=MESH,
        )

    def ring(q):
        return lax.rem(2 + 3 * q + (q // 2) * (2 * q - 1), 4)

    def peer(k):
        far_group = lax.rem(group + ring(k // 16), 4)
        far_x = lax.rem(dom // 4 + ring(lax.rem(k // 4, 4)), 4)
        far_y = lax.rem(lax.rem(dom, 4) + ring(lax.rem(k, 4)), 4)
        return far_group * 16 + far_x * 4 + far_y

    barrier = pltpu.get_barrier_semaphore()

    def greet(k, carry):
        row = peer(k)
        pl.semaphore_signal(barrier, inc=1, device_id=device(row, pen), device_id_type=MESH)
        pl.semaphore_signal(barrier, inc=1, device_id=device(row, other_chip), device_id_type=MESH)
        return carry

    lax.fori_loop(0, ROWS - 1, greet, 0)
    for k in (1, 2, 3):
        pl.semaphore_signal(
            barrier, inc=1, device_id=device(me, lax.rem(pen + k, PEN)), device_id_type=MESH
        )
    for dx in (1, ROWS - 1):
        for dy in (1, PEN - 1):
            pl.semaphore_signal(
                barrier, inc=1, device_id=device(lax.rem(me + dx, ROWS), lax.rem(pen + dy, PEN)),
                device_id_type=MESH,
            )

    for copy in first:
        copy.wait()
    halo_ref[4, 3 * TILES :, :] = jnp.where(iota((TILES, TILE), 0) < live, charges[...], 0.0)
    slab_row = slab_buf[...]
    slab_rows = slab_row.astype(F32)
    slab_cols = jnp.concatenate(
        [
            jnp.broadcast_to(slab_rows[:, half * G : (half + 1) * G], (G, G)).T
            for half in range(2)
        ],
        axis=0,
    )
    slab_cols = jnp.concatenate([slab_cols, slab_cols], axis=1)
    same = (slab_cols == slab_rows) & (iota((NLINES, NLINES), 0) < iota((NLINES, NLINES), 1))
    rank = jnp.sum(same.astype(F32), axis=0, keepdims=True).astype(jnp.int32)
    pick = (iota((ROWS * CAP, NLINES), 0) == slab_row * CAP + rank).astype(F32).astype(BF16)
    owner = jnp.where(iota((ROWS, NLINES), 0) == slab_row, target_buf[...].astype(F32), 0.0)
    place = (iota((TILE, NLINES), 0) == rank).astype(F32)
    line_iota = iota((NLINES, CHUNK), 0)
    cell_iota = iota((G, CHUNK), 0)

    def spread(chunk, total):
        where = pl.ds(pl.multiple_of(chunk * CHUNK, CHUNK), CHUNK)
        charge = jnp.concatenate(
            [
                halo_ref[4, pl.ds(3 * TILES + chunk * (CHUNK // TILE) + q, 1), :]
                for q in range(CHUNK // TILE)
            ],
            axis=1,
        )
        for corner in range(8):
            cell = cells[corner : corner + 1, where]
            high, low = split(weights[corner : corner + 1, where] * charge)
            hit = line_iota == cell // G
            lines = jnp.concatenate(
                [
                    jnp.where(hit, high.astype(F32), 0.0).astype(BF16),
                    jnp.where(hit, low.astype(F32), 0.0).astype(BF16),
                ],
                axis=0,
            )
            spots = (cell_iota == cell % G).astype(F32).astype(BF16)
            total = total + dot_nt(lines, spots)
        return total

    total = lax.fori_loop(0, TILES * TILE // CHUNK, spread, jnp.zeros((2 * NLINES, G), F32))
    lines_high, lines_low = split(total[:NLINES] + total[NLINES:])
    send_ref[:, :CAP, :] = (dot(pick, lines_high) + dot(pick, lines_low)).reshape(ROWS, CAP, G)
    send_ref[:, CAP, :] = dot_nt(owner.astype(BF16), place.astype(BF16))

    pl.semaphore_wait(barrier, 2 * (ROWS - 1) + 3 + 4)

    def send_lines(k, carry):
        row = peer(k)
        remote(
            send_ref.at[row, pl.ds(0, CAP + 1)], line_buf.at[me, pl.ds(0, CAP + 1)],
            line_sems.at[0], line_sems.at[1], row, pen,
        ).start()
        return carry

    lax.fori_loop(0, ROWS - 1, send_lines, 0)
    line_buf[me, 0 : CAP + 1, :] = send_ref[me, 0 : CAP + 1, :]

    slabs = ((rho_hbm, rho), (sus_hbm, sus), (ion_hbm, ion))

    def slab_copy(index, k):
        source, whole = slabs[index]
        return remote(
            source, whole.at[:, columns, :],
            pen_sems.at[0, index, k - 1], pen_sems.at[1, index, k - 1],
            me, lax.rem(pen + k, PEN),
        )

    for k in (1, 2, 3):
        slab_copy(0, k).start()

    neighbours = [(dx, dy) for dx in (-1, 0, 1) for dy in (-1, 0, 1) if (dx, dy) != (0, 0)]

    def halo_copy(dx, dy):
        number = (1 - dx) * 3 + 1 - dy
        return remote(
            halo_ref.at[4], halo_ref.at[number], halo_send_sems.at[number],
            halo_recv_sems.at[number],
            lax.rem(me + dx + ROWS, ROWS), lax.rem(pen + dy + PEN, PEN),
        )

    for dx, dy in neighbours:
        halo_copy(dx, dy).start()
    for copy in later:
        copy.wait()

    half = me // 32
    y_row = pen * 32 + lax.rem(me, 32)
    lam_yz = flat_ref[pl.ds(y_row, 1), :] + flat_ref[pl.ds(G + half, 1), :]
    green[...] = 1.0 / (SCREENING + (flat_ref[0:G, :] + lam_yz))

    source_of = iota((ROWS * CAP, ROWS), 0) // CAP == iota((ROWS * CAP, ROWS), 1)
    source_of = source_of.astype(F32).astype(BF16)
    own_lane = iota((ROWS * CAP, G), 1) == lax.rem(iota((ROWS * CAP, G), 0), CAP)
    for axis in range(3):
        columns_of[axis] = halo_ref[4, axis * TILES : (axis + 1) * TILES, :].T * (
            BOX_HEIGHT if axis == 2 else 1.0
        )

    def whole_line_copy(ref, sems):
        most = ref.at[pl.ds(0, ROWS - 1), pl.ds(0, CAP + 1)]
        return pltpu.make_async_remote_copy(
            src_ref=most, dst_ref=most, send_sem=sems.at[0], recv_sem=sems.at[1],
            device_id=device(lax.rem(me + 1, ROWS), pen), device_id_type=MESH,
        )

    whole_line_copy(line_buf, line_sems).wait_recv()
    spread_targets = dot(source_of, line_buf[:, CAP, :].astype(BF16))
    target = jnp.sum(jnp.where(own_lane, spread_targets, 0.0), axis=1, keepdims=True)
    landing = (target == iota((ROWS * CAP, ROWS), 1).astype(F32)).astype(F32)
    landing_t = landing.T.astype(BF16)
    landing = landing.astype(BF16)
    lines_high, lines_low = split(line_buf[:, :CAP, :].reshape(ROWS * CAP, G))
    own_mm = dot(landing_t, lines_high) + dot(landing_t, lines_low)
    for x in range(2):
        mm[x, columns, :] = own_mm[x * 32 : (x + 1) * 32]

    def mm_copy(k):
        return remote(
            mm.at[:, columns, :], mm.at[:, columns, :], mm_sems.at[0, k - 1], mm_sems.at[1, k - 1],
            me, lax.rem(pen + k, PEN),
        )

    for k in (1, 2, 3):
        mm_copy(k).start()
    for k in (1, 2, 3):
        slab_copy(0, k).wait_recv()
    for k in (1, 2, 3):
        mm_copy(k).wait_recv()

    tile_lane = iota((TILE, TILES), 1)

    def own_tile(t, carry):
        own = [
            jnp.broadcast_to(
                jnp.sum(jnp.where(tile_lane == t, columns_of[axis], 0.0), axis=1, keepdims=True),
                (TILE, TILE),
            )
            for axis in range(3)
        ]

        def partner_tile(n, total):
            chosen = nbr_ref[t, n]
            d = lax.div(chosen, TILES)
            tile = lax.rem(chosen, TILES)
            row = [halo_ref[d, pl.ds(axis * TILES + tile, 1), :] for axis in range(4)]
            row[0] = row[0] + (lax.div(d, 3) - 1).astype(F32)
            row[1] = row[1] + (lax.rem(d, 3) - 1).astype(F32)
            row[2] = row[2] * BOX_HEIGHT
            return total + pair_values(own, row)

        total = lax.fori_loop(0, NBR, partner_tile, jnp.zeros((TILE, TILE), F32))
        short[:, pl.ds(pl.multiple_of(t * TILE, TILE), TILE)] = jnp.sum(
            total.T, axis=0, keepdims=True
        )
        return carry

    def wide(index):
        return jnp.concatenate([big_ref[2 * index], big_ref[2 * index + 1]], axis=1)

    done = 0
    low_lanes = iota((ROWS, G), 1) < ROWS

    def fwd_all():
        most_send, most_recv = fwd_send.at[pl.ds(0, ROWS - 1)], fwd_recv.at[pl.ds(0, ROWS - 1)]
        return pltpu.make_async_remote_copy(
            src_ref=most_send, dst_ref=most_recv, send_sem=fwd_sems.at[0], recv_sem=fwd_sems.at[1],
            device_id=device(lax.rem(me + 1, ROWS), pen), device_id_type=MESH,
        )

    def ret_copy(slot, row, column):
        return remote(
            ret_send.at[pl.ds(row, 1)],
            ret_recv.at[slot, half, core, z_lo, pl.ds(lax.rem(me, 32), 1)],
            ret_sems.at[0], ret_sems.at[1 + slot], row, column,
        )

    def ret_all(slot):
        most = ret_send.at[pl.ds(0, 2 * ROWS - 1)]
        return pltpu.make_async_remote_copy(
            src_ref=most, dst_ref=most, send_sem=ret_sems.at[0], recv_sem=ret_sems.at[1 + slot],
            device_id=device(lax.rem(me + 1, ROWS), pen), device_id_type=MESH,
        )

    def core_copy(slot, h):
        return remote(
            ret_recv.at[slot, h, core], ret_recv.at[slot, h, core],
            core_sems.at[0, slot, h], core_sems.at[1, slot, h], me, sibling,
        )

    for iteration in range(ITERS):
        slot = iteration % 2
        source = jnp.concatenate([rho[0] + mm[0], rho[1] + mm[1]], axis=1)
        spectrum = left_const(square_ref[0, columns, :], square_ref[1, columns, :], source)
        spectrum = right_const(spectrum, wide(0), wide(1))
        if iteration > 0:
            fwd_all().wait_send()
        fwd_send[0:32, :] = spectrum[:, :G]
        fwd_send[32:64, :] = spectrum[:, G:]

        def send_fwd(k, carry):
            row = peer(k)
            remote(
                fwd_send.at[pl.ds(row, 1)], fwd_recv.at[pl.ds(me, 1)],
                fwd_sems.at[0], fwd_sems.at[1], row, pen,
            ).start()
            return carry

        lax.fori_loop(0, ROWS - 1, send_fwd, 0)
        fwd_recv[pl.ds(me, 1), :] = fwd_send[pl.ds(me, 1), :]
        if iteration == 0:
            for index in (1, 2):
                for k in (1, 2, 3):
                    slab_copy(index, k).start()
            for dx, dy in neighbours:
                halo_copy(dx, dy).wait()
            for dx, dy in neighbours:
                outside = (me + dx < 0) | (me + dx >= ROWS) | (pen + dy < 0) | (pen + dy >= PEN)

                @pl.when(outside)
                def _():
                    halo_ref[(dx + 1) * 3 + dy + 1] = jnp.zeros((4 * TILES, TILE), F32)

        lax.fori_loop(done, done + FWD_TILES, own_tile, 0)
        done += FWD_TILES
        fwd_all().wait_recv()
        received = fwd_recv[...]
        both = jnp.concatenate([received, pltpu.roll(received, ROWS, 1)], axis=0)
        modes = left_const(square_ref[4], square_ref[5], both) * green[...]
        solved = left_const(square_ref[6], square_ref[7], modes)
        if iteration > 0:
            ret_all(1 - slot).wait_send()
        ret_send[:ROWS, :] = jnp.where(low_lanes, solved[:ROWS], pltpu.roll(solved[ROWS:], ROWS, 1))

        def send_ret(k, carry):
            row = peer(k)
            ret_copy(slot, row, other_chip).start()
            ret_copy(slot, row, pen).start()
            return carry

        lax.fori_loop(0, ROWS - 1, send_ret, 0)
        ret_copy(slot, me, other_chip).start()
        ret_recv[slot, half, core, z_lo, pl.ds(lax.rem(me, 32), 1)] = ret_send[pl.ds(me, 1), :]
        lax.fori_loop(done, done + RET_TILES, own_tile, 0)
        done += RET_TILES
        ret_all(slot).wait_recv()
        for h in range(2):
            core_copy(slot, h).start()
        if iteration == 0:
            for index in (1, 2):
                for k in (1, 2, 3):
                    slab_copy(index, k).wait_recv()
        for h in range(2):
            core_copy(slot, h).wait_recv()
        lines = jnp.concatenate([ret_recv[slot, h].reshape(G, G) for h in range(2)], axis=1)
        lines = right_const(lines, wide(2), wide(3))
        potential = left_const(square_ref[2], square_ref[3], lines)
        for x in range(2):
            own = potential[:, x * G : (x + 1) * G]
            if iteration == ITERS - 1:
                last_pot[x] = own
            rho[x] = rho[x] - MIX_RATE * (rho[x] + sus[x] * (own + ion[x]))
        for h in range(2):
            core_copy(slot, h).wait_send()

    row_u = 1.0 + 2.0 * (iota((G, G), 0).astype(F32) + 0.5) / G
    lane_u = 1.0 + 2.0 * (iota((G, G), 1).astype(F32) + 0.5) / G
    x_u = [1.0 + 2.0 * ((2 * me + x).astype(F32) + 0.5) / G for x in range(2)]
    weighted = rho[0] * x_u[0] + rho[1] * x_u[1]
    plain = rho[0] + rho[1]
    sums = [weighted, plain * row_u, weighted * row_u, plain * lane_u]
    own_moments = jnp.zeros((1, G), F32)
    for index, term in enumerate(sums):
        value = jnp.sum(jnp.sum(term, axis=0, keepdims=True), axis=1, keepdims=True)
        own_moments = jnp.where(iota((1, G), 1) == index, value, own_moments)
    own_pot = jnp.concatenate([last_pot[x, columns, :] for x in range(2)], axis=0)
    pot_high, pot_low = split(own_pot)
    line_send[:, :CAP, :] = (dot(landing, pot_high) + dot(landing, pot_low)).reshape(ROWS, CAP, G)
    line_send[:, CAP, :] = jnp.broadcast_to(own_moments, (ROWS, G))

    def send_back(k, carry):
        row = peer(k)
        remote(
            line_send.at[row, pl.ds(0, CAP + 1)], back_ref.at[me, pl.ds(0, CAP + 1)],
            back_sems.at[0], back_sems.at[1], row, pen,
        ).start()
        return carry

    lax.fori_loop(0, ROWS - 1, send_back, 0)
    back_ref[me, 0 : CAP + 1, :] = line_send[me, 0 : CAP + 1, :]
    for x in range(2):
        pot_out[x] = last_pot[x, columns, :]
        rho_out[x] = rho[x, columns, :]
    lax.fori_loop(done, TILES, own_tile, 0)

    whole_line_copy(line_buf, line_sems).wait_send()
    for k in (1, 2, 3):
        for index in range(3):
            slab_copy(index, k).wait_send()
        mm_copy(k).wait_send()
    fwd_all().wait_send()
    ret_all((ITERS - 1) % 2).wait_send()
    whole_line_copy(line_send, back_sems).wait()

    back_high, back_low = split(back_ref[:, :CAP, :].reshape(ROWS * CAP, G))
    values = dot_tn(jnp.concatenate([back_high, back_low], axis=1), pick)
    values_high, values_low = split(values[:G] + values[G:])
    values = jnp.concatenate([values_high, values_low], axis=0)
    moments = jnp.sum(back_ref[:, CAP, :], axis=0, keepdims=True) * (1.0 / (G * math.sqrt(G)))
    moment = [
        jnp.sum(jnp.where(iota((1, G), 1) == m, moments, 0.0), axis=1, keepdims=True)
        for m in range(4)
    ]

    def gather(chunk, carry):
        where = pl.ds(pl.multiple_of(chunk * CHUNK, CHUNK), CHUNK)
        total = short[:, where]
        for corner in range(8):
            cell = cells[corner : corner + 1, where]
            lines = (line_iota == cell // G).astype(F32).astype(BF16)
            found = dot(values, lines)
            found = jnp.where(cell_iota == cell % G, found[:G] + found[G:], 0.0)
            total = total + weights[corner : corner + 1, where] * jnp.sum(
                found, axis=0, keepdims=True
            )
        for m in range(4):
            total = total + moment[m] * basis_ref[m : m + 1, where]
        atom = chunk * CHUNK + iota((1, CHUNK), 1)
        mm_out[:, where] = jnp.where(atom // TILE < live, total, 0.0)
        return carry

    lax.fori_loop(0, TILES * TILE // CHUNK, gather, 0)


def shards(
    atom_positions, atom_charges, multipole_basis, spread_cell, spread_weight, line_slab,
    line_target, neighbour_tiles, live_tiles, initial_density, susceptibility, ion_potential,
):
    vmem = pl.BlockSpec(memory_space=pltpu.VMEM)
    smem = pl.BlockSpec(memory_space=pltpu.SMEM)
    hbm = pl.BlockSpec(memory_space=pltpu.HBM)
    atoms = TILES * TILE
    square, big, flat = (jnp.asarray(table) for table in tables())
    block = initial_density.shape
    dma = pltpu.SemaphoreType.DMA
    buffer = pltpu.VMEM
    potential, density, values = pl.pallas_call(
        kernel,
        out_shape=(
            jax.ShapeDtypeStruct(block, F32),
            jax.ShapeDtypeStruct(block, F32),
            jax.ShapeDtypeStruct((1, atoms), F32),
        ),
        in_specs=[smem] * 2 + [hbm] * 13,
        out_specs=(vmem,) * 3,
        scratch_shapes=[
            buffer((8, atoms), jnp.int32),
            buffer((8, atoms), F32),
            buffer((TILES, TILE), F32),
            buffer((1, NLINES), jnp.int32),
            buffer((1, NLINES), jnp.int32),
            buffer((4, atoms), F32),
            buffer(square.shape, BF16),
            buffer(big.shape, BF16),
            buffer(flat.shape, F32),
            buffer((ROWS, 16, G), F32),
            buffer((ROWS, 16, G), F32),
            buffer((9, 4 * TILES, TILE), F32),
            buffer((2, G, G), F32),
            buffer((2, G, G), F32),
            buffer((2, G, G), F32),
            buffer((2, G, G), F32),
            buffer((ROWS, G), F32),
            buffer((ROWS, G), F32),
            buffer((2 * ROWS, G), F32),
            buffer((2, 2, 2, 2, 32, G), F32),
            buffer((G, G), F32),
            buffer((ROWS, 16, G), F32),
            buffer((2, G, G), F32),
            buffer((ROWS, 16, G), F32),
            buffer((3, TILE, TILES), F32),
            buffer((1, atoms), F32),
            dma((13,)),
            dma((2,)),
            dma((2, 3, 3)),
            dma((2, 3)),
            dma((9,)),
            dma((9,)),
            dma((2,)),
            dma((3,)),
            dma((2, 2, 2)),
            dma((2,)),
        ],
        compiler_params=pltpu.CompilerParams(
            collective_id=0, has_side_effects=True, vmem_limit_bytes=VMEM_LIMIT
        ),
        name="embed",
    )(
        live_tiles, neighbour_tiles[0, 0], spread_cell[0, 0], spread_weight[0, 0],
        atom_positions.reshape(3 * TILES, TILE), atom_charges.reshape(TILES, TILE),
        line_slab.reshape(1, NLINES), line_target[0], initial_density, susceptibility,
        ion_potential, multipole_basis[0, 0], square, big, flat,
    )
    return potential, density, values[None]


def solution(mesh):
    row = ("group", "dom")
    placed = (
        P(row, "pen", None, None),
        P(row, "pen", None),
        P(row, "pen", None, None),
        P(row, "pen", None, None),
        P(row, "pen", None, None),
        P(row, "pen", None, None),
        P(row, "pen", None),
        P(row, "pen", None, None),
        P(row, "pen"),
        P(row, "pen", None),
        P(row, "pen", None),
        P(row, "pen", None),
    )
    return jax.shard_map(
        shards,
        mesh=mesh,
        in_specs=placed,
        out_specs=(P(row, "pen", None), P(row, "pen", None), P(row, "pen", None)),
        check_vma=False,
    )
```

```python
import math

import jax
import jax.numpy as jnp
import ml_dtypes
import numpy as np
from jax import lax
from jax.experimental import pallas as pl
from jax.experimental.pallas import tpu as pltpu
from jax.sharding import PartitionSpec as P

MESH = pl.DeviceIdType.MESH
F32 = jnp.float32
BF16 = jnp.bfloat16
G = 128
TILE = 128
TILES = 16
NBR = 16
ITERS = 4
ROWS = 64
PEN = 4
CAP = 8
NLINES = 256
MIX_RATE = 0.3
SCREENING = 0.1
BOX_HEIGHT = 4.0
SOFTENING = 0.01
ERF_SHIFT = 1.35
ERF_POLY = (
    8.048848463632075e-05,
    0.279831566396696,
    0.40782855654035,
    0.3006583844815809,
    1.260144403309312,
    -1.158323294058104,
    2.9062706842895354,
    -1.262709002135607,
)
VMEM_LIMIT = 64 * 1024 * 1024


def halves(table):
    high = table.astype(ml_dtypes.bfloat16)
    low = (table - high.astype(np.float64)).astype(ml_dtypes.bfloat16)
    return [high, low]


def tables():
    k = np.arange(G)
    angle = 2.0 * np.pi * (np.outer(k, k) % G) / G
    cas = (np.cos(angle) + np.sin(angle)) / np.sqrt(G)
    order = np.concatenate([np.arange(32) + 32 * (2 * z + c) for c in range(2) for z in range(2)])
    split_x = np.concatenate([np.arange(ROWS) * 2, np.arange(ROWS) * 2 + 1])
    square = halves(cas) + halves(cas[:, order]) + halves(cas[:, split_x]) + halves(cas[split_x, :])
    wide = np.zeros((2, G, 2, 2, ROWS))
    for x in range(2):
        for h in range(2):
            wide[x, :, h, x, :] = cas[:, h * ROWS : (h + 1) * ROWS]
    wide = wide.reshape(2 * G, 2 * G)
    big = halves(wide) + halves(wide.T)
    lam = 2.0 - 2.0 * np.cos(2.0 * np.pi * k / G)
    lam_rows = np.repeat(lam[:, None], G, axis=1)
    lam_lanes = np.zeros((8, G))
    for h in range(2):
        lam_lanes[h] = np.tile(lam[h * ROWS : (h + 1) * ROWS], 2)
    flat = np.concatenate([lam_rows, lam_lanes]).astype(np.float32)
    big = [part[:, h * G : (h + 1) * G] for part in big for h in range(2)]
    return np.stack(square), np.stack(big), flat


def split(x):
    high = x.astype(BF16)
    return high, (x - high.astype(F32)).astype(BF16)


def dot(a, b):
    return jnp.dot(a, b, preferred_element_type=F32)


def dot_nt(a, b):
    return lax.dot_general(a, b, (((1,), (1,)), ((), ())), preferred_element_type=F32)


def dot_tn(a, b):
    return lax.dot_general(a, b, (((0,), (0,)), ((), ())), preferred_element_type=F32)


def left_const(both, x):
    rows = both.shape[0] // 2
    x_high, x_low = split(x)
    wide = dot(both, x_high)
    return wide[:rows] + (wide[rows:] + dot(both[:rows], x_low))


def right_const(x, high, low):
    rows = x.shape[0]
    x_high, x_low = split(x)
    wide = dot(jnp.concatenate([x_high, x_low], axis=0), high)
    return wide[:rows] + (wide[rows:] + dot(x_high, low))


def iota(shape, dim):
    return lax.broadcasted_iota(jnp.int32, shape, dim)


AGREE_TILES = 1
FWD_TILES = 2
RET_TILES = 1


def pair_values(own, partner):
    dx = own[0] - partner[0]
    dy = own[1] - partner[1]
    dz = own[2] - partner[2]
    s = dx * dx + dy * dy + dz * dz + SOFTENING
    u = lax.rsqrt(s)
    t = 1.0 / (s * u + ERF_SHIFT)
    poly = jnp.full_like(t, ERF_POLY[-1])
    for coefficient in ERF_POLY[-2::-1]:
        poly = poly * t + coefficient
    return (partner[3] * u) * (poly * jnp.exp(-4.0 * s))


def kernel(
    live_ref, nbr_ref, cell_hbm, weight_hbm, positions_hbm, charge_hbm, slab_hbm, target_hbm,
    rho_hbm, sus_hbm, ion_hbm, basis_hbm, square_hbm, big_hbm, flat_hbm,
    pot_out, rho_out, mm_out,
    cells, weights, charges, slab_buf, target_buf, basis_ref, square_ref, big_ref, flat_ref,
    send_ref, line_buf, halo_ref, mm, rho, sus, ion, fwd_send, fwd_recv, ret_send, ret_recv,
    green, line_send, moment_send, moment_recv, back_ref, columns_of, short,
    load_sems, line_sems, pen_sems, mm_sems, halo_send_sems, halo_recv_sems, fwd_sems, ret_sems,
    core_sems, back_sems, moment_sems,
):
    group, dom, pen = lax.axis_index("group"), lax.axis_index("dom"), lax.axis_index("pen")
    me = group * 16 + dom
    core, z_lo = lax.rem(pen, 2), pen // 2
    other_chip = lax.rem(pen + 2, PEN)
    sibling = z_lo * 2 + (1 - core)
    columns = pl.ds(pl.multiple_of(pen * 32, 32), 32)
    live = live_ref[0, 0]
    atoms = TILES * TILE

    first = [
        pltpu.make_async_copy(source, target, load_sems.at[index])
        for index, (source, target) in enumerate(
            (
                (cell_hbm, cells),
                (weight_hbm, weights),
                (charge_hbm, charges),
                (slab_hbm, slab_buf),
                (target_hbm, target_buf),
                (positions_hbm, halo_ref.at[4, pl.ds(0, 3 * TILES)]),
            )
        )
    ]
    later = [
        pltpu.make_async_copy(source, target, load_sems.at[6 + index])
        for index, (source, target) in enumerate(
            (
                (rho_hbm, rho.at[:, columns, :]),
                (sus_hbm, sus.at[:, columns, :]),
                (ion_hbm, ion.at[:, columns, :]),
                (flat_hbm, flat_ref),
                (square_hbm, square_ref),
                (big_hbm, big_ref),
                (basis_hbm, basis_ref),
            )
        )
    ]
    for copy in first:
        copy.start()

    def remote(src, dst, send_sem, recv_sem, where):
        return pltpu.make_async_remote_copy(
            src_ref=src, dst_ref=dst, send_sem=send_sem, recv_sem=recv_sem,
            device_id=where, device_id_type=MESH,
        )

    def ring(q):
        return lax.rem(2 + 3 * q + (q // 2) * (2 * q - 1), 4)

    dom_x, dom_y = dom // 4, lax.rem(dom, 4)
    ys = [lax.rem(dom_y + offset, 4) for offset in (2, 1, 3, 0)]

    def each_x(count, act):
        def step(q, carry):
            far_x = lax.rem(dom_x + ring(q), 4) * 4
            for y in ys:
                act(far_x + y)
            return carry

        lax.fori_loop(0, count, step, 0)

    def each_peer(act):
        def step(q, carry):
            far_group = lax.rem(group + ring(q // 4), 4)
            far_x = lax.rem(dom_x + ring(lax.rem(q, 4)), 4) * 4
            for y in ys:
                act(far_group, far_x + y)
            return carry

        lax.fori_loop(0, 15, step, 0)
        for y in ys[:3]:
            act(group, dom_x * 4 + y)

    barrier = pltpu.get_barrier_semaphore()

    def signal(*where):
        pl.semaphore_signal(barrier, inc=1, device_id=where, device_id_type=MESH)

    def greet(far_group, far_dom):
        signal(far_group, far_dom, pen)
        signal(far_group, far_dom, other_chip)

    each_peer(greet)
    for k in (1, 2, 3):
        signal(group, dom, lax.rem(pen + k, PEN))
    for dx in (1, ROWS - 1):
        for dy in (1, PEN - 1):
            row = lax.rem(me + dx, ROWS)
            signal(row // 16, lax.rem(row, 16), lax.rem(pen + dy, PEN))

    for copy in later:
        copy.start()

    for copy in first:
        copy.wait()
    halo_ref[4, 3 * TILES :, :] = jnp.where(iota((TILES, TILE), 0) < live, charges[...], 0.0)
    slab_row = slab_buf[...]
    slab_rows = slab_row.astype(F32)
    slab_cols = jnp.concatenate(
        [
            jnp.broadcast_to(slab_rows[:, half * G : (half + 1) * G], (G, G)).T
            for half in range(2)
        ],
        axis=0,
    )
    slab_cols = jnp.concatenate([slab_cols, slab_cols], axis=1)
    same = (slab_cols == slab_rows) & (iota((NLINES, NLINES), 0) < iota((NLINES, NLINES), 1))
    rank = jnp.sum(same.astype(F32), axis=0, keepdims=True).astype(jnp.int32)
    pick = (iota((ROWS * CAP, NLINES), 0) == slab_row * CAP + rank).astype(F32)
    pick, pick_t = pick.astype(BF16), pick.T.astype(BF16)
    owner = jnp.where(iota((ROWS, NLINES), 0) == slab_row, target_buf[...].astype(F32), 0.0)
    place = (iota((TILE, NLINES), 0) == rank).astype(F32)
    one, zero = jnp.ones((), BF16), jnp.zeros((), BF16)
    line_iota = iota((NLINES, atoms), 0).astype(F32).astype(BF16)
    cell_iota = iota((G, atoms), 0).astype(F32).astype(BF16)
    charge = jnp.concatenate(
        [halo_ref[4, 3 * TILES + t : 3 * TILES + t + 1, :] for t in range(TILES)], axis=1
    )

    def lines_of(corner):
        cell = cells[corner : corner + 1, :]
        line = lax.div(cell, G).astype(F32).astype(BF16)
        return cell, jnp.where(line_iota == line, one, zero)

    total = jnp.zeros((2 * G, NLINES), F32)
    for corner in range(8):
        cell, lines = lines_of(corner)
        high, low = split(weights[corner : corner + 1, :] * charge)
        hit = cell_iota == lax.rem(cell, G).astype(F32).astype(BF16)
        spots = jnp.concatenate([jnp.where(hit, high, zero), jnp.where(hit, low, zero)], axis=0)
        total = total + dot_nt(spots, lines)
    lines_high, lines_low = split(total[:G] + total[G:])
    send_ref[:, :CAP, :] = (dot_nt(pick, lines_high) + dot_nt(pick, lines_low)).reshape(
        ROWS, CAP, G
    )
    send_ref[:, CAP, :] = dot_nt(owner.astype(BF16), place.astype(BF16))

    pl.semaphore_wait(barrier, 2 * (ROWS - 1) + 3 + 4)

    def send_lines(far_group, far_dom):
        remote(
            send_ref.at[far_group * 16 + far_dom, pl.ds(0, CAP + 1)],
            line_buf.at[me, pl.ds(0, CAP + 1)],
            line_sems.at[0], line_sems.at[1], (far_group, far_dom, pen),
        ).start()

    each_peer(send_lines)
    line_buf[me, 0 : CAP + 1, :] = send_ref[me, 0 : CAP + 1, :]

    slabs = ((rho_hbm, rho), (sus_hbm, sus), (ion_hbm, ion))

    def slab_copy(index, k):
        source, whole = slabs[index]
        return remote(
            source, whole.at[:, columns, :],
            pen_sems.at[0, index, k - 1], pen_sems.at[1, index, k - 1],
            (group, dom, lax.rem(pen + k, PEN)),
        )

    for k in (1, 2, 3):
        slab_copy(0, k).start()

    neighbours = [(dx, dy) for dx in (-1, 0, 1) for dy in (-1, 0, 1) if (dx, dy) != (0, 0)]

    def halo_copy(dx, dy):
        number = (1 - dx) * 3 + 1 - dy
        row = lax.rem(me + dx + ROWS, ROWS)
        return remote(
            halo_ref.at[4], halo_ref.at[number], halo_send_sems.at[number],
            halo_recv_sems.at[number],
            (row // 16, lax.rem(row, 16), lax.rem(pen + dy + PEN, PEN)),
        )

    for dx, dy in neighbours:
        halo_copy(dx, dy).start()
    for copy in later:
        copy.wait()

    half = me // 32
    y_row = pen * 32 + lax.rem(me, 32)
    lam_yz = flat_ref[pl.ds(y_row, 1), :] + flat_ref[pl.ds(G + half, 1), :]
    green[...] = 1.0 / (SCREENING + (flat_ref[0:G, :] + lam_yz))

    source_of = iota((ROWS * CAP, ROWS), 0) // CAP == iota((ROWS * CAP, ROWS), 1)
    source_of = source_of.astype(F32).astype(BF16)
    own_lane = iota((ROWS * CAP, G), 1) == lax.rem(iota((ROWS * CAP, G), 0), CAP)
    for axis in range(3):
        columns_of[axis] = halo_ref[4, axis * TILES : (axis + 1) * TILES, :].T * (
            BOX_HEIGHT if axis == 2 else 1.0
        )

    def all_of(ref, send_sem, recv_sem):
        return remote(ref, ref, send_sem, recv_sem, (group, dom, sibling))

    def all_lines():
        most = line_buf.at[pl.ds(0, ROWS - 1), pl.ds(0, CAP + 1)]
        return all_of(most, line_sems.at[0], line_sems.at[1])

    all_lines().wait_recv()
    spread_targets = dot(source_of, line_buf[:, CAP, :].astype(BF16))
    target = jnp.sum(jnp.where(own_lane, spread_targets, 0.0), axis=1, keepdims=True)
    landing = (target == iota((ROWS * CAP, ROWS), 1).astype(F32)).astype(F32)
    landing_t = landing.T.astype(BF16)
    landing = landing.astype(BF16)
    lines_high, lines_low = split(line_buf[:, :CAP, :].reshape(ROWS * CAP, G))
    own_mm = dot(landing_t, lines_high) + dot(landing_t, lines_low)
    for x in range(2):
        mm[x, columns, :] = own_mm[x * 32 : (x + 1) * 32]

    def mm_copy(k):
        return remote(
            mm.at[:, columns, :], mm.at[:, columns, :], mm_sems.at[0, k - 1], mm_sems.at[1, k - 1],
            (group, dom, lax.rem(pen + k, PEN)),
        )

    for k in (1, 2, 3):
        mm_copy(k).start()
    tile_lane = iota((TILE, TILES), 1)

    def own_tile(t, carry):
        own = [
            jnp.broadcast_to(
                jnp.sum(jnp.where(tile_lane == t, columns_of[axis], 0.0), axis=1, keepdims=True),
                (TILE, TILE),
            )
            for axis in range(3)
        ]

        def partner_tile(n, total):
            chosen = nbr_ref[t, n]
            d = lax.div(chosen, TILES)
            tile = lax.rem(chosen, TILES)
            row = [halo_ref[d, pl.ds(axis * TILES + tile, 1), :] for axis in range(4)]
            row[0] = row[0] + (lax.div(d, 3) - 1).astype(F32)
            row[1] = row[1] + (lax.rem(d, 3) - 1).astype(F32)
            row[2] = row[2] * BOX_HEIGHT
            return total + pair_values(own, row)

        total = lax.fori_loop(0, NBR, partner_tile, jnp.zeros((TILE, TILE), F32))
        short[:, pl.ds(pl.multiple_of(t * TILE, TILE), TILE)] = jnp.sum(
            total.T, axis=0, keepdims=True
        )
        return carry

    for dx, dy in neighbours:
        halo_copy(dx, dy).wait()
    for dx, dy in neighbours:
        outside = (me + dx < 0) | (me + dx >= ROWS) | (pen + dy < 0) | (pen + dy >= PEN)

        @pl.when(outside)
        def _():
            halo_ref[(dx + 1) * 3 + dy + 1] = jnp.zeros((4 * TILES, TILE), F32)

    lax.fori_loop(0, AGREE_TILES, own_tile, 0)
    done = AGREE_TILES
    for k in (1, 2, 3):
        slab_copy(0, k).wait_recv()
    for k in (1, 2, 3):
        mm_copy(k).wait_recv()

    def square(index):
        return jnp.concatenate([square_ref[2 * index], square_ref[2 * index + 1]], axis=0)

    def wide(index):
        return jnp.concatenate([big_ref[2 * index], big_ref[2 * index + 1]], axis=1)

    low_lanes = iota((ROWS, G), 1) < ROWS

    y_rows = [pl.ds(pl.multiple_of((2 * z + core) * 32, 32), 32) for z in range(2)]
    y_table = jnp.concatenate([square_ref[part, rows, :] for part in range(2) for rows in y_rows])
    across, beside = lax.rem(group + 2, 4), lax.rem(group + 3 - 2 * z_lo, 4)

    def fwd_copy(far_group, far_dom, z):
        return remote(
            fwd_send.at[z, pl.ds(far_group * 16 + far_dom, 1)], fwd_recv.at[pl.ds(me, 1)],
            fwd_sems.at[0], fwd_sems.at[1], (far_group, far_dom, 2 * z + core),
        )

    def fwd_all():
        return all_of(fwd_recv.at[pl.ds(0, ROWS - 1)], fwd_sems.at[0], fwd_sems.at[1])

    def ret_copy(slot, far_group, far_dom, column):
        return remote(
            ret_send.at[pl.ds(far_group * 16 + far_dom, 1)],
            ret_recv.at[slot, half, core, z_lo, pl.ds(lax.rem(me, 32), 1)],
            ret_sems.at[0], ret_sems.at[1 + slot], (far_group, far_dom, column),
        )

    def ret_all(slot):
        return all_of(ret_send.at[pl.ds(0, 2 * ROWS - 1)], ret_sems.at[0], ret_sems.at[1 + slot])

    def core_copy(slot, h):
        return remote(
            ret_recv.at[slot, h, core], ret_recv.at[slot, h, core],
            core_sems.at[0, slot, h], core_sems.at[1, slot, h], (group, dom, sibling),
        )

    def back_copy(far_group, far_dom):
        return remote(
            line_send.at[far_group * 16 + far_dom], back_ref.at[me],
            back_sems.at[0], back_sems.at[1], (far_group, far_dom, pen),
        )

    def moment_copy(far_group, far_dom):
        return remote(
            moment_send, moment_recv.at[pl.ds(me, 1)],
            moment_sems.at[0], moment_sems.at[1], (far_group, far_dom, pen),
        )

    for iteration in range(ITERS):
        slot = iteration % 2
        source = jnp.concatenate([rho[0] + mm[0], rho[1] + mm[1]], axis=1)
        spectrum = right_const(left_const(y_table, source), wide(0), wide(1))
        if iteration > 0:
            fwd_all().wait_send()
        for z in range(2):
            for h in range(2):
                fwd_send[z, h * 32 : (h + 1) * 32, :] = spectrum[
                    z * 32 : (z + 1) * 32, h * G : (h + 1) * G
                ]

        def send_across(far_dom):
            fwd_copy(across, far_dom, 1 - z_lo).start()

        def send_beside(far_dom):
            fwd_copy(beside, far_dom, 1 - z_lo).start()
            fwd_copy(beside, far_dom, z_lo).start()

        def send_near(far_dom):
            fwd_copy(group, far_dom, z_lo).start()

        each_x(4, send_across)
        each_x(4, send_beside)
        each_x(3, send_near)
        for y in ys[:3]:
            send_near(dom_x * 4 + y)
        fwd_recv[pl.ds(me, 1), :] = fwd_send[z_lo, pl.ds(me, 1), :]
        if iteration == 0:
            for index in (1, 2):
                for k in (1, 2, 3):
                    slab_copy(index, k).start()
        lax.fori_loop(done, done + FWD_TILES, own_tile, 0)
        done += FWD_TILES
        fwd_all().wait_recv()
        received = fwd_recv[...]
        both = jnp.concatenate([received, pltpu.roll(received, ROWS, 1)], axis=0)
        modes = left_const(square(2), both) * green[...]
        solved = left_const(square(3), modes)
        if iteration > 0:
            ret_all(1 - slot).wait_send()
        ret_send[:ROWS, :] = jnp.where(low_lanes, solved[:ROWS], pltpu.roll(solved[ROWS:], ROWS, 1))

        def send_ret(far_group, far_dom):
            ret_copy(slot, far_group, far_dom, other_chip).start()
            ret_copy(slot, far_group, far_dom, pen).start()

        each_peer(send_ret)
        ret_copy(slot, group, dom, other_chip).start()
        ret_recv[slot, half, core, z_lo, pl.ds(lax.rem(me, 32), 1)] = ret_send[pl.ds(me, 1), :]
        lax.fori_loop(done, done + RET_TILES, own_tile, 0)
        done += RET_TILES
        ret_all(slot).wait_recv()
        for h in range(2):
            core_copy(slot, h).start()
        if iteration == 0:
            for index in (1, 2):
                for k in (1, 2, 3):
                    slab_copy(index, k).wait_recv()
        for h in range(2):
            core_copy(slot, h).wait_recv()
        lines = jnp.concatenate([ret_recv[slot, h].reshape(G, G) for h in range(2)], axis=1)
        lines = right_const(lines, wide(2), wide(3))
        if iteration == ITERS - 1:
            own_table = jnp.concatenate([square_ref[part, columns, :] for part in (2, 3)])
            own_pot = left_const(own_table, lines)
            own_pot = jnp.concatenate([own_pot[:, x * G : (x + 1) * G] for x in range(2)], axis=0)
            pot_high, pot_low = split(own_pot)
            line_send[...] = (dot(landing, pot_high) + dot(landing, pot_low)).reshape(ROWS, CAP, G)
            each_peer(lambda far_group, far_dom: back_copy(far_group, far_dom).start())
            back_ref[me] = line_send[me]
        potential = left_const(square(1), lines)
        for x in range(2):
            own = potential[:, x * G : (x + 1) * G]
            rho[x] = rho[x] - MIX_RATE * (rho[x] + sus[x] * (own + ion[x]))
        for h in range(2):
            core_copy(slot, h).wait_send()

    row_u = 1.0 + 2.0 * (iota((G, G), 0).astype(F32) + 0.5) / G
    lane_u = 1.0 + 2.0 * (iota((G, G), 1).astype(F32) + 0.5) / G
    x_u = [1.0 + 2.0 * ((2 * me + x).astype(F32) + 0.5) / G for x in range(2)]
    weighted = rho[0] * x_u[0] + rho[1] * x_u[1]
    plain = rho[0] + rho[1]
    sums = [weighted, plain * row_u, weighted * row_u, plain * lane_u]
    own_moments = jnp.zeros((1, G), F32)
    for index, term in enumerate(sums):
        value = jnp.sum(jnp.sum(term, axis=0, keepdims=True), axis=1, keepdims=True)
        own_moments = jnp.where(iota((1, G), 1) == index, value, own_moments)
    moment_send[...] = own_moments
    each_peer(lambda far_group, far_dom: moment_copy(far_group, far_dom).start())
    moment_recv[pl.ds(me, 1), :] = own_moments
    for x in range(2):
        pot_out[x] = own_pot[x * 32 : (x + 1) * 32]
        rho_out[x] = rho[x, columns, :]
    lax.fori_loop(done, TILES, own_tile, 0)

    all_lines().wait_send()
    for k in (1, 2, 3):
        for index in range(3):
            slab_copy(index, k).wait_send()
        mm_copy(k).wait_send()
    fwd_all().wait_send()
    ret_all((ITERS - 1) % 2).wait_send()
    all_of(moment_recv.at[pl.ds(0, ROWS - 1)], moment_sems.at[0], moment_sems.at[1]).wait()
    all_of(back_ref.at[pl.ds(0, ROWS - 1)], back_sems.at[0], back_sems.at[1]).wait()

    back_high, back_low = split(back_ref[...].reshape(ROWS * CAP, G))
    values_high, values_low = split((dot(pick_t, back_high) + dot(pick_t, back_low)).T)
    values = jnp.concatenate([values_high, values_low], axis=0)
    moments = jnp.sum(moment_recv[...], axis=0, keepdims=True) * (1.0 / (G * math.sqrt(G)))
    moment = [
        jnp.sum(jnp.where(iota((1, G), 1) == m, moments, 0.0), axis=1, keepdims=True)
        for m in range(4)
    ]

    spot_iota = iota((G, atoms), 0)
    found = jnp.zeros((G, atoms), F32)
    for corner in range(8):
        cell, lines = lines_of(corner)
        weight = jnp.where(spot_iota == lax.rem(cell, G), weights[corner : corner + 1, :], 0.0)
        halves_found = dot(values, lines)
        found = found + weight * (halves_found[:G] + halves_found[G:])
    total = short[...] + jnp.sum(found, axis=0, keepdims=True)
    for m in range(4):
        total = total + moment[m] * basis_ref[m : m + 1, :]
    mm_out[...] = jnp.where(lax.div(iota((1, atoms), 1), TILE) < live, total, 0.0)


def shards(
    atom_positions, atom_charges, multipole_basis, spread_cell, spread_weight, line_slab,
    line_target, neighbour_tiles, live_tiles, initial_density, susceptibility, ion_potential,
):
    vmem = pl.BlockSpec(memory_space=pltpu.VMEM)
    smem = pl.BlockSpec(memory_space=pltpu.SMEM)
    hbm = pl.BlockSpec(memory_space=pltpu.HBM)
    atoms = TILES * TILE
    square, big, flat = (jnp.asarray(table) for table in tables())
    block = initial_density.shape
    dma = pltpu.SemaphoreType.DMA
    buffer = pltpu.VMEM
    potential, density, values = pl.pallas_call(
        kernel,
        out_shape=(
            jax.ShapeDtypeStruct(block, F32),
            jax.ShapeDtypeStruct(block, F32),
            jax.ShapeDtypeStruct((1, atoms), F32),
        ),
        in_specs=[smem] * 2 + [hbm] * 13,
        out_specs=(vmem,) * 3,
        scratch_shapes=[
            buffer((8, atoms), jnp.int32),
            buffer((8, atoms), F32),
            buffer((TILES, TILE), F32),
            buffer((1, NLINES), jnp.int32),
            buffer((1, NLINES), jnp.int32),
            buffer((4, atoms), F32),
            buffer(square.shape, BF16),
            buffer(big.shape, BF16),
            buffer(flat.shape, F32),
            buffer((ROWS, 16, G), F32),
            buffer((ROWS, 16, G), F32),
            buffer((9, 4 * TILES, TILE), F32),
            buffer((2, G, G), F32),
            buffer((2, G, G), F32),
            buffer((2, G, G), F32),
            buffer((2, G, G), F32),
            buffer((2, ROWS, G), F32),
            buffer((ROWS, G), F32),
            buffer((2 * ROWS, G), F32),
            buffer((2, 2, 2, 2, 32, G), F32),
            buffer((G, G), F32),
            buffer((ROWS, CAP, G), F32),
            buffer((1, G), F32),
            buffer((ROWS, G), F32),
            buffer((ROWS, CAP, G), F32),
            buffer((3, TILE, TILES), F32),
            buffer((1, atoms), F32),
            dma((13,)),
            dma((2,)),
            dma((2, 3, 3)),
            dma((2, 3)),
            dma((9,)),
            dma((9,)),
            dma((2,)),
            dma((3,)),
            dma((2, 2, 2)),
            dma((2,)),
            dma((2,)),
        ],
        compiler_params=pltpu.CompilerParams(
            collective_id=0, has_side_effects=True, vmem_limit_bytes=VMEM_LIMIT
        ),
        name="embed",
    )(
        live_tiles, neighbour_tiles[0, 0], spread_cell[0, 0], spread_weight[0, 0],
        atom_positions.reshape(3 * TILES, TILE), atom_charges.reshape(TILES, TILE),
        line_slab.reshape(1, NLINES), line_target[0], initial_density, susceptibility,
        ion_potential, multipole_basis[0, 0], square, big, flat,
    )
    return potential, density, values[None]


def solution(mesh):
    row = ("group", "dom")
    placed = (
        P(row, "pen", None, None),
        P(row, "pen", None),
        P(row, "pen", None, None),
        P(row, "pen", None, None),
        P(row, "pen", None, None),
        P(row, "pen", None, None),
        P(row, "pen", None),
        P(row, "pen", None, None),
        P(row, "pen"),
        P(row, "pen", None),
        P(row, "pen", None),
        P(row, "pen", None),
    )
    return jax.shard_map(
        shards,
        mesh=mesh,
        in_specs=placed,
        out_specs=(P(row, "pen", None), P(row, "pen", None), P(row, "pen", None)),
        check_vma=False,
    )
```

```python
import math

import jax
import jax.numpy as jnp
import ml_dtypes
import numpy as np
from jax import lax
from jax.experimental import pallas as pl
from jax.experimental.pallas import tpu as pltpu
from jax.sharding import PartitionSpec as P

MESH = pl.DeviceIdType.MESH
F32 = jnp.float32
BF16 = jnp.bfloat16
G = 128
TILE = 128
TILES = 16
NBR = 16
ITERS = 4
ROWS = 64
PEN = 4
CAP = 8
NLINES = 256
MIX_RATE = 0.3
SCREENING = 0.1
BOX_HEIGHT = 4.0
SOFTENING = 0.01
ERF_SHIFT = 1.35
ERF_POLY = (
    8.048848463632075e-05,
    0.279831566396696,
    0.40782855654035,
    0.3006583844815809,
    1.260144403309312,
    -1.158323294058104,
    2.9062706842895354,
    -1.262709002135607,
)
VMEM_LIMIT = 64 * 1024 * 1024


def halves(table):
    high = table.astype(ml_dtypes.bfloat16)
    low = (table - high.astype(np.float64)).astype(ml_dtypes.bfloat16)
    return [high, low]


def tables():
    k = np.arange(G)
    angle = 2.0 * np.pi * (np.outer(k, k) % G) / G
    cas = (np.cos(angle) + np.sin(angle)) / np.sqrt(G)
    order = np.concatenate([np.arange(32) + 32 * (2 * z + c) for c in range(2) for z in range(2)])
    split_x = np.concatenate([np.arange(ROWS) * 2, np.arange(ROWS) * 2 + 1])
    square = halves(cas) + halves(cas[:, order]) + halves(cas[:, split_x]) + halves(cas[split_x, :])
    wide = np.zeros((2, G, 2, 2, ROWS))
    for x in range(2):
        for h in range(2):
            wide[x, :, h, x, :] = cas[:, h * ROWS : (h + 1) * ROWS]
    wide = wide.reshape(2 * G, 2 * G)
    big = halves(wide) + halves(wide.T)
    lam = 2.0 - 2.0 * np.cos(2.0 * np.pi * k / G)
    lam_rows = np.repeat(lam[:, None], G, axis=1)
    lam_lanes = np.zeros((8, G))
    for h in range(2):
        lam_lanes[h] = np.tile(lam[h * ROWS : (h + 1) * ROWS], 2)
    flat = np.concatenate([lam_rows, lam_lanes]).astype(np.float32)
    big = [part[:, h * G : (h + 1) * G] for part in big for h in range(2)]
    return np.stack(square), np.stack(big), flat


def split(x):
    high = x.astype(BF16)
    return high, (x - high.astype(F32)).astype(BF16)


def dot(a, b):
    return jnp.dot(a, b, preferred_element_type=F32)


def dot_nt(a, b):
    return lax.dot_general(a, b, (((1,), (1,)), ((), ())), preferred_element_type=F32)


def dot_tn(a, b):
    return lax.dot_general(a, b, (((0,), (0,)), ((), ())), preferred_element_type=F32)


def left_const(both, x):
    rows = both.shape[0] // 2
    x_high, x_low = split(x)
    wide = dot(both, x_high)
    return wide[:rows] + (wide[rows:] + dot(both[:rows], x_low))


def right_const(x, high, low):
    rows = x.shape[0]
    x_high, x_low = split(x)
    wide = dot(jnp.concatenate([x_high, x_low], axis=0), high)
    return wide[:rows] + (wide[rows:] + dot(x_high, low))


def iota(shape, dim):
    return lax.broadcasted_iota(jnp.int32, shape, dim)


FWD_TILES = (2, 2, 2, 2)
RET_TILES = (2, 2, 2, 1)


def pair_values(own, partner):
    dx = own[0] - partner[0]
    dy = own[1] - partner[1]
    dz = own[2] - partner[2]
    s = dx * dx + dy * dy + dz * dz + SOFTENING
    u = lax.rsqrt(s)
    t = 1.0 / (s * u + ERF_SHIFT)
    poly = jnp.full_like(t, ERF_POLY[-1])
    for coefficient in ERF_POLY[-2::-1]:
        poly = poly * t + coefficient
    return (partner[3] * u) * (poly * jnp.exp(-4.0 * s))


def kernel(
    live_ref, nbr_hbm, cell_hbm, weight_hbm, positions_hbm, charge_hbm, slab_hbm, target_hbm,
    rho_hbm, sus_hbm, ion_hbm, basis_hbm, square_hbm, big_hbm, flat_hbm,
    pot_out, rho_out, mm_out,
    cells, weights, charges, slab_buf, target_buf, basis_ref, square_ref, big_ref, flat_ref,
    send_ref, line_buf, halo_ref, mm, rho, sus, ion, fwd_send, fwd_recv, ret_send, ret_recv,
    green, line_send, moment_send, moment_recv, back_ref, columns_of, short,
    load_sems, line_sems, pen_sems, mm_sems, halo_send_sems, halo_recv_sems, fwd_sems, ret_sems,
    core_sems, back_sems, moment_sems, line_table, weight_table, pot_buf, out_sems,
    nbr_ref,
):
    group, dom, pen = lax.axis_index("group"), lax.axis_index("dom"), lax.axis_index("pen")
    me = group * 16 + dom
    core, z_lo = lax.rem(pen, 2), pen // 2
    other_chip = lax.rem(pen + 2, PEN)
    sibling = z_lo * 2 + (1 - core)
    columns = pl.ds(pl.multiple_of(pen * 32, 32), 32)
    atoms = TILES * TILE

    first = [
        pltpu.make_async_copy(source, target, load_sems.at[index])
        for index, (source, target) in enumerate(
            (
                (cell_hbm, cells),
                (weight_hbm, weights),
                (charge_hbm, charges),
                (slab_hbm, slab_buf),
                (target_hbm, target_buf),
                (positions_hbm, halo_ref.at[4, pl.ds(0, 3 * TILES)]),
            )
        )
    ]
    later = [
        pltpu.make_async_copy(source, target, load_sems.at[6 + index])
        for index, (source, target) in enumerate(
            (
                (rho_hbm, rho.at[:, columns, :]),
                (sus_hbm, sus.at[:, columns, :]),
                (ion_hbm, ion.at[:, columns, :]),
                (flat_hbm, flat_ref),
                (square_hbm, square_ref),
                (big_hbm, big_ref),
                (basis_hbm, basis_ref),
                (nbr_hbm, nbr_ref),
            )
        )
    ]
    for copy in first:
        copy.start()

    def remote(src, dst, send_sem, recv_sem, where):
        return pltpu.make_async_remote_copy(
            src_ref=src, dst_ref=dst, send_sem=send_sem, recv_sem=recv_sem,
            device_id=where, device_id_type=MESH,
        )

    def ring(q):
        return lax.rem(2 + 3 * q + (q // 2) * (2 * q - 1), 4)

    dom_x, dom_y = dom // 4, lax.rem(dom, 4)
    offsets = (2, 1, 3, 0)
    doms = [
        lax.rem(dom_x + x, 4) * 4 + lax.rem(dom_y + y, 4) for x in offsets for y in offsets
    ]

    def each_peer(act):
        def step(q, carry):
            far_group = lax.rem(group + ring(q), 4)
            for far_dom in doms:
                act(far_group, far_dom)
            return carry

        lax.fori_loop(0, 3, step, 0)
        for far_dom in doms[:15]:
            act(group, far_dom)

    barrier = pltpu.get_barrier_semaphore()

    def signal(*where):
        pl.semaphore_signal(barrier, inc=1, device_id=where, device_id_type=MESH)

    def greet(far_group, far_dom):
        signal(far_group, far_dom, pen)
        signal(far_group, far_dom, other_chip)

    each_peer(greet)
    for k in (1, 2, 3):
        signal(group, dom, lax.rem(pen + k, PEN))
    for dx in (1, ROWS - 1):
        for dy in (1, PEN - 1):
            row = lax.rem(me + dx, ROWS)
            signal(row // 16, lax.rem(row, 16), lax.rem(pen + dy, PEN))

    for copy in later:
        copy.start()

    for copy in first:
        copy.wait()
    live = live_ref[0, 0]
    halo_ref[4, 3 * TILES :, :] = jnp.where(iota((TILES, TILE), 0) < live, charges[...], 0.0)
    slab_row = slab_buf[...]
    slab_rows = slab_row.astype(F32)
    slab_cols = jnp.concatenate(
        [
            jnp.broadcast_to(slab_rows[:, half * G : (half + 1) * G], (G, G)).T
            for half in range(2)
        ],
        axis=0,
    )
    slab_cols = jnp.concatenate([slab_cols, slab_cols], axis=1)
    same = (slab_cols == slab_rows) & (iota((NLINES, NLINES), 0) < iota((NLINES, NLINES), 1))
    rank = jnp.sum(same.astype(F32), axis=0, keepdims=True).astype(jnp.int32)
    pick = (iota((ROWS * CAP, NLINES), 0) == slab_row * CAP + rank).astype(F32)
    pick_high = pick.astype(BF16)
    owner = jnp.where(iota((ROWS, NLINES), 0) == slab_row, target_buf[...].astype(F32), 0.0)
    place = (iota((TILE, NLINES), 0) == rank).astype(F32)
    one, zero = jnp.ones((), BF16), jnp.zeros((), BF16)
    line_iota = iota((NLINES, atoms), 0).astype(F32).astype(BF16)
    cell_iota = iota((G, atoms), 0).astype(F32).astype(BF16)
    charge = jnp.concatenate(
        [halo_ref[4, 3 * TILES + t : 3 * TILES + t + 1, :] for t in range(TILES)], axis=1
    )

    def lines_of(corner):
        cell = cells[corner : corner + 1, :]
        line = lax.div(cell, G).astype(F32).astype(BF16)
        return cell, jnp.where(line_iota == line, one, zero)

    total = jnp.zeros((2 * G, NLINES), F32)
    for corner in range(8):
        cell, lines = lines_of(corner)
        line_table[corner] = lines
        high, low = split(weights[corner : corner + 1, :] * charge)
        hit = cell_iota == lax.rem(cell, G).astype(F32).astype(BF16)
        spots = jnp.concatenate([jnp.where(hit, high, zero), jnp.where(hit, low, zero)], axis=0)
        total = total + dot_nt(spots, lines)
    lines_high, lines_low = split(total[:G] + total[G:])
    send_ref[:, :CAP, :] = (dot_nt(pick_high, lines_high) + dot_nt(pick_high, lines_low)).reshape(
        ROWS, CAP, G
    )
    send_ref[:, CAP, :] = dot_nt(owner.astype(BF16), place.astype(BF16))

    pl.semaphore_wait(barrier, 2 * (ROWS - 1) + 3 + 4)

    def send_lines(far_group, far_dom):
        remote(
            send_ref.at[far_group * 16 + far_dom, pl.ds(0, CAP + 1)],
            line_buf.at[me, pl.ds(0, CAP + 1)],
            line_sems.at[0], line_sems.at[1], (far_group, far_dom, pen),
        ).start()

    each_peer(send_lines)
    line_buf[me, 0 : CAP + 1, :] = send_ref[me, 0 : CAP + 1, :]

    slabs = ((rho_hbm, rho), (sus_hbm, sus), (ion_hbm, ion))

    def slab_copy(index, k):
        source, whole = slabs[index]
        return remote(
            source, whole.at[:, columns, :],
            pen_sems.at[0, index, k - 1], pen_sems.at[1, index, k - 1],
            (group, dom, lax.rem(pen + k, PEN)),
        )

    for k in (1, 2, 3):
        slab_copy(0, k).start()

    neighbours = [(dx, dy) for dx in (-1, 0, 1) for dy in (-1, 0, 1) if (dx, dy) != (0, 0)]

    def halo_copy(dx, dy):
        number = (1 - dx) * 3 + 1 - dy
        row = lax.rem(me + dx + ROWS, ROWS)
        return remote(
            halo_ref.at[4], halo_ref.at[number], halo_send_sems.at[number],
            halo_recv_sems.at[number],
            (row // 16, lax.rem(row, 16), lax.rem(pen + dy + PEN, PEN)),
        )

    for dx, dy in neighbours:
        halo_copy(dx, dy).start()
    for copy in later:
        copy.wait()

    half = me // 32
    y_row = pen * 32 + lax.rem(me, 32)
    lam_yz = flat_ref[pl.ds(y_row, 1), :] + flat_ref[pl.ds(G + half, 1), :]
    green[...] = 1.0 / (SCREENING + (flat_ref[0:G, :] + lam_yz))

    pick_t = pick.T.astype(BF16)

    source_of = iota((ROWS * CAP, ROWS), 0) // CAP == iota((ROWS * CAP, ROWS), 1)
    source_of = source_of.astype(F32).astype(BF16)
    own_lane = iota((ROWS * CAP, G), 1) == lax.rem(iota((ROWS * CAP, G), 0), CAP)
    for axis in range(3):
        columns_of[axis] = halo_ref[4, axis * TILES : (axis + 1) * TILES, :].T * (
            BOX_HEIGHT if axis == 2 else 1.0
        )

    def all_of(ref, send_sem, recv_sem):
        return remote(ref, ref, send_sem, recv_sem, (group, dom, sibling))

    def all_lines():
        most = line_buf.at[pl.ds(0, ROWS - 1), pl.ds(0, CAP + 1)]
        return all_of(most, line_sems.at[0], line_sems.at[1])

    all_lines().wait_recv()
    targets = line_buf[:, CAP, :]
    targets_t = jnp.concatenate([targets, targets], axis=0).T
    line_of_row = iota((ROWS, ROWS), 0).astype(F32)
    landing_t = jnp.concatenate(
        [(targets_t[k : k + 1, :ROWS] == line_of_row).astype(F32) for k in range(CAP)], axis=1
    ).astype(BF16)
    received = jnp.concatenate([line_buf[:, k, :] for k in range(CAP)], axis=0)
    lines_high, lines_low = split(received)
    own_mm = dot(landing_t, lines_high) + dot(landing_t, lines_low)
    for x in range(2):
        mm[x, columns, :] = own_mm[x * 32 : (x + 1) * 32]

    def mm_copy(k):
        return remote(
            mm.at[:, columns, :], mm.at[:, columns, :], mm_sems.at[0, k - 1], mm_sems.at[1, k - 1],
            (group, dom, lax.rem(pen + k, PEN)),
        )

    for k in (1, 2, 3):
        mm_copy(k).start()
    spread_targets = dot(source_of, targets.astype(BF16))
    target = jnp.sum(jnp.where(own_lane, spread_targets, 0.0), axis=1, keepdims=True)
    landing = (target == iota((ROWS * CAP, ROWS), 1).astype(F32)).astype(F32).astype(BF16)
    tile_lane = iota((TILE, TILES), 1)

    def own_tile(t, carry):
        own = [
            jnp.broadcast_to(
                jnp.sum(jnp.where(tile_lane == t, columns_of[axis], 0.0), axis=1, keepdims=True),
                (TILE, TILE),
            )
            for axis in range(3)
        ]

        def partner_tile(n, total):
            chosen = nbr_ref[t, n]
            d = lax.div(chosen, TILES)
            tile = lax.rem(chosen, TILES)
            row = [halo_ref[d, pl.ds(axis * TILES + tile, 1), :] for axis in range(4)]
            row[0] = row[0] + (lax.div(d, 3) - 1).astype(F32)
            row[1] = row[1] + (lax.rem(d, 3) - 1).astype(F32)
            row[2] = row[2] * BOX_HEIGHT
            return total + pair_values(own, row)

        total = lax.fori_loop(0, NBR, partner_tile, jnp.zeros((TILE, TILE), F32))
        short[:, pl.ds(pl.multiple_of(t * TILE, TILE), TILE)] = jnp.sum(
            total.T, axis=0, keepdims=True
        )
        return carry

    for dx, dy in neighbours:
        halo_copy(dx, dy).wait()
    for dx, dy in neighbours:
        outside = (me + dx < 0) | (me + dx >= ROWS) | (pen + dy < 0) | (pen + dy >= PEN)

        @pl.when(outside)
        def _():
            halo_ref[(dx + 1) * 3 + dy + 1] = jnp.zeros((4 * TILES, TILE), F32)

    done = 0
    for k in (1, 2, 3):
        slab_copy(0, k).wait_recv()
    for k in (1, 2, 3):
        mm_copy(k).wait_recv()

    def square(index):
        return jnp.concatenate([square_ref[2 * index], square_ref[2 * index + 1]], axis=0)

    def wide(index):
        return jnp.concatenate([big_ref[2 * index], big_ref[2 * index + 1]], axis=1)

    low_lanes = iota((ROWS, G), 1) < ROWS

    y_rows = [pl.ds(pl.multiple_of((2 * z + core) * 32, 32), 32) for z in range(2)]
    y_table = jnp.concatenate([square_ref[part, rows, :] for part in range(2) for rows in y_rows])
    across, beside = lax.rem(group + 2, 4), lax.rem(group + 3 - 2 * z_lo, 4)

    def fwd_copy(far_group, far_dom, z):
        return remote(
            fwd_send.at[z, pl.ds(far_group * 16 + far_dom, 1)], fwd_recv.at[pl.ds(me, 1)],
            fwd_sems.at[0], fwd_sems.at[1], (far_group, far_dom, 2 * z + core),
        )

    def fwd_all():
        return all_of(fwd_recv.at[pl.ds(0, ROWS - 1)], fwd_sems.at[0], fwd_sems.at[1])

    def ret_copy(slot, far_group, far_dom, column):
        return remote(
            ret_send.at[pl.ds(far_group * 16 + far_dom, 1)],
            ret_recv.at[slot, half, core, z_lo, pl.ds(lax.rem(me, 32), 1)],
            ret_sems.at[0], ret_sems.at[1 + slot], (far_group, far_dom, column),
        )

    def ret_all(slot):
        return all_of(ret_send.at[pl.ds(0, 2 * ROWS - 1)], ret_sems.at[0], ret_sems.at[1 + slot])

    def core_copy(slot, h):
        return remote(
            ret_recv.at[slot, h, core], ret_recv.at[slot, h, core],
            core_sems.at[0, slot, h], core_sems.at[1, slot, h], (group, dom, sibling),
        )

    def back_copy(far_group, far_dom):
        return remote(
            line_send.at[far_group * 16 + far_dom], back_ref.at[me],
            back_sems.at[0], back_sems.at[1], (far_group, far_dom, pen),
        )

    def moment_copy(far_group, far_dom):
        return remote(
            moment_send, moment_recv.at[pl.ds(me, 1)],
            moment_sems.at[0], moment_sems.at[1], (far_group, far_dom, pen),
        )

    for iteration in range(ITERS):
        slot = iteration % 2
        source = jnp.concatenate([rho[0] + mm[0], rho[1] + mm[1]], axis=1)
        spectrum = right_const(left_const(y_table, source), wide(0), wide(1))
        if iteration > 0:
            fwd_all().wait_send()
        for z in range(2):
            for h in range(2):
                fwd_send[z, h * 32 : (h + 1) * 32, :] = spectrum[
                    z * 32 : (z + 1) * 32, h * G : (h + 1) * G
                ]

        def send_across(far_dom):
            fwd_copy(across, far_dom, 1 - z_lo).start()

        def send_beside(far_dom):
            fwd_copy(beside, far_dom, 1 - z_lo).start()
            fwd_copy(beside, far_dom, z_lo).start()

        def send_near(far_dom):
            fwd_copy(group, far_dom, z_lo).start()

        for far_dom in doms:
            send_across(far_dom)
        for far_dom in doms:
            send_beside(far_dom)
        for far_dom in doms[:15]:
            send_near(far_dom)
        fwd_recv[pl.ds(me, 1), :] = fwd_send[z_lo, pl.ds(me, 1), :]
        if iteration == 0:
            for index in (1, 2):
                for k in (1, 2, 3):
                    slab_copy(index, k).start()
        lax.fori_loop(done, done + FWD_TILES[iteration], own_tile, 0)
        done += FWD_TILES[iteration]
        fwd_all().wait_recv()
        received = fwd_recv[...]
        both = jnp.concatenate([received, pltpu.roll(received, ROWS, 1)], axis=0)
        modes = left_const(square(2), both) * green[...]
        solved = left_const(square(3), modes)
        if iteration > 0:
            ret_all(1 - slot).wait_send()
        ret_send[:ROWS, :] = jnp.where(low_lanes, solved[:ROWS], pltpu.roll(solved[ROWS:], ROWS, 1))

        def send_ret(far_group, far_dom):
            ret_copy(slot, far_group, far_dom, other_chip).start()
            ret_copy(slot, far_group, far_dom, pen).start()

        each_peer(send_ret)
        ret_copy(slot, group, dom, other_chip).start()
        ret_recv[slot, half, core, z_lo, pl.ds(lax.rem(me, 32), 1)] = ret_send[pl.ds(me, 1), :]
        lax.fori_loop(done, done + RET_TILES[iteration], own_tile, 0)
        done += RET_TILES[iteration]
        ret_all(slot).wait_recv()
        for h in range(2):
            core_copy(slot, h).start()
        if iteration == 0:
            for index in (1, 2):
                for k in (1, 2, 3):
                    slab_copy(index, k).wait_recv()
        for h in range(2):
            core_copy(slot, h).wait_recv()
        lines = jnp.concatenate([ret_recv[slot, h].reshape(G, G) for h in range(2)], axis=1)
        lines = right_const(lines, wide(2), wide(3))
        if iteration == ITERS - 1:
            own_table = jnp.concatenate([square_ref[part, columns, :] for part in (2, 3)])
            own_pot = left_const(own_table, lines)
            own_pot = jnp.concatenate([own_pot[:, x * G : (x + 1) * G] for x in range(2)], axis=0)
            pot_high, pot_low = split(own_pot)
            line_send[...] = (dot(landing, pot_high) + dot(landing, pot_low)).reshape(ROWS, CAP, G)
            each_peer(lambda far_group, far_dom: back_copy(far_group, far_dom).start())
            back_ref[me] = line_send[me]
        potential = left_const(square(1), lines)
        for x in range(2):
            own = potential[:, x * G : (x + 1) * G]
            rho[x] = rho[x] - MIX_RATE * (rho[x] + sus[x] * (own + ion[x]))
        for h in range(2):
            core_copy(slot, h).wait_send()

    row_u = 1.0 + 2.0 * (iota((G, G), 0).astype(F32) + 0.5) / G
    lane_u = 1.0 + 2.0 * (iota((G, G), 1).astype(F32) + 0.5) / G
    x_u = [1.0 + 2.0 * ((2 * me + x).astype(F32) + 0.5) / G for x in range(2)]
    weighted = rho[0] * x_u[0] + rho[1] * x_u[1]
    plain = rho[0] + rho[1]
    sums = [weighted, plain * row_u, weighted * row_u, plain * lane_u]
    own_moments = jnp.zeros((1, G), F32)
    for index, term in enumerate(sums):
        value = jnp.sum(jnp.sum(term, axis=0, keepdims=True), axis=1, keepdims=True)
        own_moments = jnp.where(iota((1, G), 1) == index, value, own_moments)
    moment_send[...] = own_moments
    each_peer(lambda far_group, far_dom: moment_copy(far_group, far_dom).start())
    moment_recv[pl.ds(me, 1), :] = own_moments
    for x in range(2):
        pot_buf[x] = own_pot[x * 32 : (x + 1) * 32]
    stores = [
        pltpu.make_async_copy(pot_buf, pot_out, out_sems.at[0]),
        pltpu.make_async_copy(rho.at[:, columns, :], rho_out, out_sems.at[1]),
    ]
    for copy in stores:
        copy.start()
    lax.fori_loop(done, TILES, own_tile, 0)
    spot_iota = iota((G, atoms), 0)
    for corner in range(8):
        spot = lax.rem(cells[corner : corner + 1, :], G)
        weight_table[corner] = jnp.where(spot_iota == spot, weights[corner : corner + 1, :], 0.0)

    all_lines().wait_send()
    for k in (1, 2, 3):
        for index in range(3):
            slab_copy(index, k).wait_send()
        mm_copy(k).wait_send()
    fwd_all().wait_send()
    ret_all((ITERS - 1) % 2).wait_send()
    all_of(moment_recv.at[pl.ds(0, ROWS - 1)], moment_sems.at[0], moment_sems.at[1]).wait()
    all_of(back_ref.at[pl.ds(0, ROWS - 1)], back_sems.at[0], back_sems.at[1]).wait()

    back_high, back_low = split(back_ref[...].reshape(ROWS * CAP, G))
    values_high, values_low = split((dot(pick_t, back_high) + dot(pick_t, back_low)).T)
    values = jnp.concatenate([values_high, values_low], axis=0)
    moments = jnp.sum(moment_recv[...], axis=0, keepdims=True) * (1.0 / (G * math.sqrt(G)))
    moment = [
        jnp.sum(jnp.where(iota((1, G), 1) == m, moments, 0.0), axis=1, keepdims=True)
        for m in range(4)
    ]

    found = jnp.zeros((G, atoms), F32)
    for corner in range(8):
        halves_found = dot(values, line_table[corner])
        found = found + weight_table[corner] * (halves_found[:G] + halves_found[G:])
    total = short[...] + jnp.sum(found, axis=0, keepdims=True)
    for m in range(4):
        total = total + moment[m] * basis_ref[m : m + 1, :]
    mm_out[...] = jnp.where(lax.div(iota((1, atoms), 1), TILE) < live, total, 0.0)
    for copy in stores:
        copy.wait()


def copy_kernel(*refs):
    for source, target in zip(refs[:3], refs[3:]):
        target[...] = source[...]


def shards(
    atom_positions, atom_charges, multipole_basis, spread_cell, spread_weight, line_slab,
    line_target, neighbour_tiles, live_tiles, initial_density, susceptibility, ion_potential,
):
    vmem = pl.BlockSpec(memory_space=pltpu.VMEM)
    hbm = pl.BlockSpec(memory_space=pltpu.HBM)
    atoms = TILES * TILE
    square, big, flat = (jnp.asarray(table) for table in tables())
    block = initial_density.shape
    dma = pltpu.SemaphoreType.DMA
    buffer = pltpu.VMEM
    potential, density, values = pl.pallas_call(
        kernel,
        out_shape=(
            jax.ShapeDtypeStruct(block, F32),
            jax.ShapeDtypeStruct(block, F32),
            jax.ShapeDtypeStruct((1, atoms), F32),
        ),
        in_specs=[pl.BlockSpec(memory_space=pltpu.SMEM)] + [hbm] * 14,
        out_specs=(hbm, hbm, vmem),
        scratch_shapes=[
            buffer((8, atoms), jnp.int32),
            buffer((8, atoms), F32),
            buffer((TILES, TILE), F32),
            buffer((1, NLINES), jnp.int32),
            buffer((1, NLINES), jnp.int32),
            buffer((4, atoms), F32),
            buffer(square.shape, BF16),
            buffer(big.shape, BF16),
            buffer(flat.shape, F32),
            buffer((ROWS, 16, G), F32),
            buffer((ROWS, 16, G), F32),
            buffer((9, 4 * TILES, TILE), F32),
            buffer((2, G, G), F32),
            buffer((2, G, G), F32),
            buffer((2, G, G), F32),
            buffer((2, G, G), F32),
            buffer((2, ROWS, G), F32),
            buffer((ROWS, G), F32),
            buffer((2 * ROWS, G), F32),
            buffer((2, 2, 2, 2, 32, G), F32),
            buffer((G, G), F32),
            buffer((ROWS, CAP, G), F32),
            buffer((1, G), F32),
            buffer((ROWS, G), F32),
            buffer((ROWS, CAP, G), F32),
            buffer((3, TILE, TILES), F32),
            buffer((1, atoms), F32),
            dma((14,)),
            dma((2,)),
            dma((2, 3, 3)),
            dma((2, 3)),
            dma((9,)),
            dma((9,)),
            dma((2,)),
            dma((3,)),
            dma((2, 2, 2)),
            dma((2,)),
            dma((2,)),
            buffer((8, NLINES, atoms), BF16),
            buffer((8, G, atoms), F32),
            buffer((2, 32, G), F32),
            dma((2,)),
            pltpu.SMEM((TILES, NBR), jnp.int32),
        ],
        compiler_params=pltpu.CompilerParams(
            collective_id=0, has_side_effects=True, vmem_limit_bytes=VMEM_LIMIT
        ),
        name="embed",
    )(
        live_tiles, neighbour_tiles[0, 0], spread_cell[0, 0], spread_weight[0, 0],
        atom_positions.reshape(3 * TILES, TILE), atom_charges.reshape(TILES, TILE),
        line_slab.reshape(1, NLINES), line_target[0], initial_density, susceptibility,
        ion_potential, multipole_basis[0, 0], square, big, flat,
    )
    results = (potential, density, values)
    potential, density, values = pl.pallas_call(
        copy_kernel,
        out_shape=tuple(jax.ShapeDtypeStruct(r.shape, F32) for r in results),
        in_specs=[vmem] * 3,
        out_specs=(vmem,) * 3,
        name="results",
    )(*results)
    return potential, density, values[None]


def solution(mesh):
    row = ("group", "dom")
    placed = (
        P(row, "pen", None, None),
        P(row, "pen", None),
        P(row, "pen", None, None),
        P(row, "pen", None, None),
        P(row, "pen", None, None),
        P(row, "pen", None, None),
        P(row, "pen", None),
        P(row, "pen", None, None),
        P(row, "pen"),
        P(row, "pen", None),
        P(row, "pen", None),
        P(row, "pen", None),
    )
    return jax.shard_map(
        shards,
        mesh=mesh,
        in_specs=placed,
        out_specs=(P(row, "pen", None), P(row, "pen", None), P(row, "pen", None)),
        check_vma=False,
    )
```

```python
import math

import jax
import jax.numpy as jnp
import ml_dtypes
import numpy as np
from jax import lax
from jax.experimental import pallas as pl
from jax.experimental.pallas import tpu as pltpu
from jax.sharding import PartitionSpec as P

MESH = pl.DeviceIdType.MESH
F32 = jnp.float32
BF16 = jnp.bfloat16
G = 128
TILE = 128
TILES = 16
NBR = 16
ITERS = 4
ROWS = 64
PEN = 4
CAP = 8
NLINES = 256
MIX_RATE = 0.3
SCREENING = 0.1
BOX_HEIGHT = 4.0
SOFTENING = 0.01
ERF_SHIFT = 1.35
ERF_POLY = (
    8.048848463632075e-05,
    0.279831566396696,
    0.40782855654035,
    0.3006583844815809,
    1.260144403309312,
    -1.158323294058104,
    2.9062706842895354,
    -1.262709002135607,
)
VMEM_LIMIT = 64 * 1024 * 1024


def halves(table):
    high = table.astype(ml_dtypes.bfloat16)
    low = (table - high.astype(np.float64)).astype(ml_dtypes.bfloat16)
    return [high, low]


def tables():
    k = np.arange(G)
    angle = 2.0 * np.pi * (np.outer(k, k) % G) / G
    cas = (np.cos(angle) + np.sin(angle)) / np.sqrt(G)
    order = np.concatenate([np.arange(32) + 32 * (2 * z + c) for c in range(2) for z in range(2)])
    split_x = np.concatenate([np.arange(ROWS) * 2, np.arange(ROWS) * 2 + 1])
    square = halves(cas) + halves(cas[:, order]) + halves(cas[:, split_x]) + halves(cas[split_x, :])
    wide = np.zeros((2, G, 2, 2, ROWS))
    for x in range(2):
        for h in range(2):
            wide[x, :, h, x, :] = cas[:, h * ROWS : (h + 1) * ROWS]
    wide = wide.reshape(2 * G, 2 * G)
    big = halves(wide) + halves(wide.T)
    lam = 2.0 - 2.0 * np.cos(2.0 * np.pi * k / G)
    lam_rows = np.repeat(lam[:, None], G, axis=1)
    lam_lanes = np.zeros((8, G))
    for h in range(2):
        lam_lanes[h] = np.tile(lam[h * ROWS : (h + 1) * ROWS], 2)
    flat = np.concatenate([lam_rows, lam_lanes]).astype(np.float32)
    big = [part[:, h * G : (h + 1) * G] for part in big for h in range(2)]
    return np.stack(square), np.stack(big), flat


def split(x):
    high = x.astype(BF16)
    return high, (x - high.astype(F32)).astype(BF16)


def dot(a, b):
    return jnp.dot(a, b, preferred_element_type=F32)


def dot_nt(a, b):
    return lax.dot_general(a, b, (((1,), (1,)), ((), ())), preferred_element_type=F32)


def dot_tn(a, b):
    return lax.dot_general(a, b, (((0,), (0,)), ((), ())), preferred_element_type=F32)


def left_const(both, x):
    rows = both.shape[0] // 2
    x_high, x_low = split(x)
    wide = dot(both, x_high)
    return wide[:rows] + (wide[rows:] + dot(both[:rows], x_low))


def right_const(x, high, low):
    rows = x.shape[0]
    x_high, x_low = split(x)
    wide = dot(jnp.concatenate([x_high, x_low], axis=0), high)
    return wide[:rows] + (wide[rows:] + dot(x_high, low))


def iota(shape, dim):
    return lax.broadcasted_iota(jnp.int32, shape, dim)


FWD_TILES = (0, 2, 2, 2)
RET_TILES = (2, 2, 2, 2)


def pair_values(own, partner):
    dx = own[0] - partner[0]
    dy = own[1] - partner[1]
    dz = own[2] - partner[2]
    s = dx * dx + dy * dy + dz * dz + SOFTENING
    u = lax.rsqrt(s)
    t = 1.0 / (s * u + ERF_SHIFT)
    poly = jnp.full_like(t, ERF_POLY[-1])
    for coefficient in ERF_POLY[-2::-1]:
        poly = poly * t + coefficient
    return (partner[3] * u) * (poly * jnp.exp(-4.0 * s))


def kernel(
    live_ref, nbr_hbm, cell_hbm, weight_hbm, positions_hbm, charge_hbm, slab_hbm, target_hbm,
    rho_hbm, sus_hbm, ion_hbm, basis_hbm, square_hbm, big_hbm, flat_hbm,
    pot_out, rho_out, mm_out,
    cells, weights, charges, slab_buf, target_buf, basis_ref, square_ref, big_ref, flat_ref,
    send_ref, line_buf, halo_ref, mm, rho, sus, ion, fwd_send, fwd_recv, ret_send, ret_recv,
    green, line_send, moment_send, moment_recv, back_ref, columns_of, short,
    load_sems, line_sems, pen_sems, mm_sems, halo_send_sems, halo_recv_sems, fwd_sems, ret_sems,
    core_sems, back_sems, moment_sems, line_table, weight_table, pot_buf, out_sems,
    nbr_ref,
):
    group, dom, pen = lax.axis_index("group"), lax.axis_index("dom"), lax.axis_index("pen")
    me = group * 16 + dom
    core, z_lo = lax.rem(pen, 2), pen // 2
    other_chip = lax.rem(pen + 2, PEN)
    sibling = z_lo * 2 + (1 - core)
    columns = pl.ds(pl.multiple_of(pen * 32, 32), 32)
    atoms = TILES * TILE

    first = [
        pltpu.make_async_copy(source, target, load_sems.at[index])
        for index, (source, target) in enumerate(
            (
                (cell_hbm, cells),
                (weight_hbm, weights),
                (charge_hbm, charges),
                (slab_hbm, slab_buf),
                (target_hbm, target_buf),
                (positions_hbm, halo_ref.at[4, pl.ds(0, 3 * TILES)]),
            )
        )
    ]
    later = [
        pltpu.make_async_copy(source, target, load_sems.at[6 + index])
        for index, (source, target) in enumerate(
            (
                (rho_hbm, rho.at[:, columns, :]),
                (sus_hbm, sus.at[:, columns, :]),
                (ion_hbm, ion.at[:, columns, :]),
                (flat_hbm, flat_ref),
                (square_hbm, square_ref),
                (big_hbm, big_ref),
                (basis_hbm, basis_ref),
                (nbr_hbm, nbr_ref),
            )
        )
    ]
    for copy in first:
        copy.start()

    def remote(src, dst, send_sem, recv_sem, where):
        return pltpu.make_async_remote_copy(
            src_ref=src, dst_ref=dst, send_sem=send_sem, recv_sem=recv_sem,
            device_id=where, device_id_type=MESH,
        )

    def ring(q):
        return lax.rem(2 + 3 * q + (q // 2) * (2 * q - 1), 4)

    dom_x, dom_y = dom // 4, lax.rem(dom, 4)
    offsets = (2, 1, 3, 0)
    doms = [
        lax.rem(dom_x + x, 4) * 4 + lax.rem(dom_y + y, 4) for x in offsets for y in offsets
    ]

    def each_peer(act):
        def step(q, carry):
            far_group = lax.rem(group + ring(q), 4)
            for far_dom in doms:
                act(far_group, far_dom)
            return carry

        lax.fori_loop(0, 3, step, 0)
        for far_dom in doms[:15]:
            act(group, far_dom)

    barrier = pltpu.get_barrier_semaphore()

    def signal(*where):
        pl.semaphore_signal(barrier, inc=1, device_id=where, device_id_type=MESH)

    def greet(far_group, far_dom):
        signal(far_group, far_dom, pen)
        signal(far_group, far_dom, other_chip)

    each_peer(greet)
    for k in (1, 2, 3):
        signal(group, dom, lax.rem(pen + k, PEN))
    for dx in (1, ROWS - 1):
        for dy in (1, PEN - 1):
            row = lax.rem(me + dx, ROWS)
            signal(row // 16, lax.rem(row, 16), lax.rem(pen + dy, PEN))

    for copy in later:
        copy.start()

    for copy in first:
        copy.wait()
    live = live_ref[0, 0]
    halo_ref[4, 3 * TILES :, :] = jnp.where(iota((TILES, TILE), 0) < live, charges[...], 0.0)
    slab_row = slab_buf[...]
    slab_rows = slab_row.astype(F32)
    slab_cols = jnp.concatenate(
        [
            jnp.broadcast_to(slab_rows[:, half * G : (half + 1) * G], (G, G)).T
            for half in range(2)
        ],
        axis=0,
    )
    slab_cols = jnp.concatenate([slab_cols, slab_cols], axis=1)
    same = (slab_cols == slab_rows) & (iota((NLINES, NLINES), 0) < iota((NLINES, NLINES), 1))
    rank = jnp.sum(same.astype(F32), axis=0, keepdims=True).astype(jnp.int32)
    pick = (iota((ROWS * CAP, NLINES), 0) == slab_row * CAP + rank).astype(F32)
    pick_high = pick.astype(BF16)
    owner = jnp.where(iota((ROWS, NLINES), 0) == slab_row, target_buf[...].astype(F32), 0.0)
    place = (iota((TILE, NLINES), 0) == rank).astype(F32)
    one, zero = jnp.ones((), BF16), jnp.zeros((), BF16)
    line_iota = iota((NLINES, atoms), 0).astype(F32).astype(BF16)
    cell_iota = iota((G, atoms), 0).astype(F32).astype(BF16)
    charge = jnp.concatenate(
        [halo_ref[4, 3 * TILES + t : 3 * TILES + t + 1, :] for t in range(TILES)], axis=1
    )

    def lines_of(corner):
        cell = cells[corner : corner + 1, :]
        line = lax.div(cell, G).astype(F32).astype(BF16)
        return cell, jnp.where(line_iota == line, one, zero)

    total = jnp.zeros((2 * G, NLINES), F32)
    for corner in range(8):
        cell, lines = lines_of(corner)
        line_table[corner] = lines
        high, low = split(weights[corner : corner + 1, :] * charge)
        hit = cell_iota == lax.rem(cell, G).astype(F32).astype(BF16)
        spots = jnp.concatenate([jnp.where(hit, high, zero), jnp.where(hit, low, zero)], axis=0)
        total = total + dot_nt(spots, lines)
    lines_high, lines_low = split(total[:G] + total[G:])
    send_ref[:, :CAP, :] = (dot_nt(pick_high, lines_high) + dot_nt(pick_high, lines_low)).reshape(
        ROWS, CAP, G
    )
    send_ref[:, CAP, :] = dot_nt(owner.astype(BF16), place.astype(BF16))

    pl.semaphore_wait(barrier, 2 * (ROWS - 1) + 3 + 4)

    slabs = ((rho_hbm, rho), (sus_hbm, sus), (ion_hbm, ion))

    def slab_copy(index, k):
        source, whole = slabs[index]
        return remote(
            source, whole.at[:, columns, :],
            pen_sems.at[0, index, k - 1], pen_sems.at[1, index, k - 1],
            (group, dom, lax.rem(pen + k, PEN)),
        )

    for k in (1, 2, 3):
        slab_copy(0, k).start()

    def send_lines(far_group, far_dom):
        remote(
            send_ref.at[far_group * 16 + far_dom, pl.ds(0, CAP + 1)],
            line_buf.at[me, pl.ds(0, CAP + 1)],
            line_sems.at[0], line_sems.at[1], (far_group, far_dom, pen),
        ).start()

    each_peer(send_lines)
    line_buf[me, 0 : CAP + 1, :] = send_ref[me, 0 : CAP + 1, :]

    neighbours = [(dx, dy) for dx in (-1, 0, 1) for dy in (-1, 0, 1) if (dx, dy) != (0, 0)]

    def halo_copy(dx, dy):
        number = (1 - dx) * 3 + 1 - dy
        row = lax.rem(me + dx + ROWS, ROWS)
        return remote(
            halo_ref.at[4], halo_ref.at[number], halo_send_sems.at[number],
            halo_recv_sems.at[number],
            (row // 16, lax.rem(row, 16), lax.rem(pen + dy + PEN, PEN)),
        )

    for copy in later:
        copy.wait()

    half = me // 32
    y_row = pen * 32 + lax.rem(me, 32)
    lam_yz = flat_ref[pl.ds(y_row, 1), :] + flat_ref[pl.ds(G + half, 1), :]
    green[...] = 1.0 / (SCREENING + (flat_ref[0:G, :] + lam_yz))

    pick_t = pick.T.astype(BF16)

    source_of = iota((ROWS * CAP, ROWS), 0) // CAP == iota((ROWS * CAP, ROWS), 1)
    source_of = source_of.astype(F32).astype(BF16)
    own_lane = iota((ROWS * CAP, G), 1) == lax.rem(iota((ROWS * CAP, G), 0), CAP)
    for axis in range(3):
        columns_of[axis] = halo_ref[4, axis * TILES : (axis + 1) * TILES, :].T * (
            BOX_HEIGHT if axis == 2 else 1.0
        )

    def all_of(ref, send_sem, recv_sem):
        return remote(ref, ref, send_sem, recv_sem, (group, dom, sibling))

    def all_lines():
        most = line_buf.at[pl.ds(0, ROWS - 1), pl.ds(0, CAP + 1)]
        return all_of(most, line_sems.at[0], line_sems.at[1])

    all_lines().wait_recv()
    targets = line_buf[:, CAP, :]
    targets_t = jnp.concatenate([targets, targets], axis=0).T
    line_of_row = iota((ROWS, ROWS), 0).astype(F32)
    landing_t = jnp.concatenate(
        [(targets_t[k : k + 1, :ROWS] == line_of_row).astype(F32) for k in range(CAP)], axis=1
    ).astype(BF16)
    received = jnp.concatenate([line_buf[:, k, :] for k in range(CAP)], axis=0)
    lines_high, lines_low = split(received)
    own_mm = dot(landing_t, lines_high) + dot(landing_t, lines_low)
    for x in range(2):
        mm[x, columns, :] = own_mm[x * 32 : (x + 1) * 32]

    def mm_copy(k):
        return remote(
            mm.at[:, columns, :], mm.at[:, columns, :], mm_sems.at[0, k - 1], mm_sems.at[1, k - 1],
            (group, dom, lax.rem(pen + k, PEN)),
        )

    for k in (1, 2, 3):
        mm_copy(k).start()
    spread_targets = dot(source_of, targets.astype(BF16))
    target = jnp.sum(jnp.where(own_lane, spread_targets, 0.0), axis=1, keepdims=True)
    landing = (target == iota((ROWS * CAP, ROWS), 1).astype(F32)).astype(F32).astype(BF16)
    tile_lane = iota((TILE, TILES), 1)

    def own_tile(t, carry):
        own = [
            jnp.broadcast_to(
                jnp.sum(jnp.where(tile_lane == t, columns_of[axis], 0.0), axis=1, keepdims=True),
                (TILE, TILE),
            )
            for axis in range(3)
        ]

        def partner_tile(n, total):
            chosen = nbr_ref[t, n]
            d = lax.div(chosen, TILES)
            tile = lax.rem(chosen, TILES)
            row = [halo_ref[d, pl.ds(axis * TILES + tile, 1), :] for axis in range(4)]
            row[0] = row[0] + (lax.div(d, 3) - 1).astype(F32)
            row[1] = row[1] + (lax.rem(d, 3) - 1).astype(F32)
            row[2] = row[2] * BOX_HEIGHT
            return total + pair_values(own, row)

        total = lax.fori_loop(0, NBR, partner_tile, jnp.zeros((TILE, TILE), F32))
        short[:, pl.ds(pl.multiple_of(t * TILE, TILE), TILE)] = jnp.sum(
            total.T, axis=0, keepdims=True
        )
        return carry

    done = 0
    for k in (1, 2, 3):
        slab_copy(0, k).wait_recv()
    for k in (1, 2, 3):
        mm_copy(k).wait_recv()

    def square(index):
        return jnp.concatenate([square_ref[2 * index], square_ref[2 * index + 1]], axis=0)

    def wide(index):
        return jnp.concatenate([big_ref[2 * index], big_ref[2 * index + 1]], axis=1)

    low_lanes = iota((ROWS, G), 1) < ROWS

    y_rows = [pl.ds(pl.multiple_of((2 * z + core) * 32, 32), 32) for z in range(2)]
    y_table = jnp.concatenate([square_ref[part, rows, :] for part in range(2) for rows in y_rows])
    across, beside = lax.rem(group + 2, 4), lax.rem(group + 3 - 2 * z_lo, 4)

    def fwd_copy(far_group, far_dom, z):
        return remote(
            fwd_send.at[z, pl.ds(far_group * 16 + far_dom, 1)], fwd_recv.at[pl.ds(me, 1)],
            fwd_sems.at[0], fwd_sems.at[1], (far_group, far_dom, 2 * z + core),
        )

    def fwd_all():
        return all_of(fwd_recv.at[pl.ds(0, ROWS - 1)], fwd_sems.at[0], fwd_sems.at[1])

    def ret_copy(slot, far_group, far_dom, column):
        return remote(
            ret_send.at[pl.ds(far_group * 16 + far_dom, 1)],
            ret_recv.at[slot, half, core, z_lo, pl.ds(lax.rem(me, 32), 1)],
            ret_sems.at[0], ret_sems.at[1 + slot], (far_group, far_dom, column),
        )

    def ret_all(slot):
        return all_of(ret_send.at[pl.ds(0, 2 * ROWS - 1)], ret_sems.at[0], ret_sems.at[1 + slot])

    def core_copy(slot, h):
        return remote(
            ret_recv.at[slot, h, core], ret_recv.at[slot, h, core],
            core_sems.at[0, slot, h], core_sems.at[1, slot, h], (group, dom, sibling),
        )

    def back_copy(far_group, far_dom):
        return remote(
            line_send.at[far_group * 16 + far_dom], back_ref.at[me],
            back_sems.at[0], back_sems.at[1], (far_group, far_dom, pen),
        )

    def moment_copy(far_group, far_dom):
        return remote(
            moment_send, moment_recv.at[pl.ds(me, 1)],
            moment_sems.at[0], moment_sems.at[1], (far_group, far_dom, pen),
        )

    for iteration in range(ITERS):
        slot = iteration % 2
        source = jnp.concatenate([rho[0] + mm[0], rho[1] + mm[1]], axis=1)
        spectrum = right_const(left_const(y_table, source), wide(0), wide(1))
        if iteration > 0:
            fwd_all().wait_send()
        for z in range(2):
            for h in range(2):
                fwd_send[z, h * 32 : (h + 1) * 32, :] = spectrum[
                    z * 32 : (z + 1) * 32, h * G : (h + 1) * G
                ]

        def send_across(far_dom):
            fwd_copy(across, far_dom, 1 - z_lo).start()

        def send_beside(far_dom):
            fwd_copy(beside, far_dom, 1 - z_lo).start()
            fwd_copy(beside, far_dom, z_lo).start()

        def send_near(far_dom):
            fwd_copy(group, far_dom, z_lo).start()

        for far_dom in doms:
            send_across(far_dom)
        for far_dom in doms:
            send_beside(far_dom)
        for far_dom in doms[:15]:
            send_near(far_dom)
        fwd_recv[pl.ds(me, 1), :] = fwd_send[z_lo, pl.ds(me, 1), :]
        if iteration == 0:
            for dx, dy in neighbours:
                halo_copy(dx, dy).start()
            for index in (1, 2):
                for k in (1, 2, 3):
                    slab_copy(index, k).start()
        lax.fori_loop(done, done + FWD_TILES[iteration], own_tile, 0)
        done += FWD_TILES[iteration]
        fwd_all().wait_recv()
        received = fwd_recv[...]
        both = jnp.concatenate([received, pltpu.roll(received, ROWS, 1)], axis=0)
        modes = left_const(square(2), both) * green[...]
        solved = left_const(square(3), modes)
        if iteration > 0:
            ret_all(1 - slot).wait_send()
        ret_send[:ROWS, :] = jnp.where(low_lanes, solved[:ROWS], pltpu.roll(solved[ROWS:], ROWS, 1))

        def send_ret(far_group, far_dom):
            ret_copy(slot, far_group, far_dom, other_chip).start()
            ret_copy(slot, far_group, far_dom, pen).start()

        each_peer(send_ret)
        ret_copy(slot, group, dom, other_chip).start()
        ret_recv[slot, half, core, z_lo, pl.ds(lax.rem(me, 32), 1)] = ret_send[pl.ds(me, 1), :]
        if iteration == 0:
            for dx, dy in neighbours:
                halo_copy(dx, dy).wait()
            for dx, dy in neighbours:
                outside = (me + dx < 0) | (me + dx >= ROWS) | (pen + dy < 0) | (pen + dy >= PEN)

                @pl.when(outside)
                def _():
                    halo_ref[(dx + 1) * 3 + dy + 1] = jnp.zeros((4 * TILES, TILE), F32)

        lax.fori_loop(done, done + RET_TILES[iteration], own_tile, 0)
        done += RET_TILES[iteration]
        ret_all(slot).wait_recv()
        for h in range(2):
            core_copy(slot, h).start()
        if iteration == 0:
            for index in (1, 2):
                for k in (1, 2, 3):
                    slab_copy(index, k).wait_recv()
        for h in range(2):
            core_copy(slot, h).wait_recv()
        lines = jnp.concatenate([ret_recv[slot, h].reshape(G, G) for h in range(2)], axis=1)
        lines = right_const(lines, wide(2), wide(3))
        if iteration == ITERS - 1:
            own_table = jnp.concatenate([square_ref[part, columns, :] for part in (2, 3)])
            own_pot = left_const(own_table, lines)
            own_pot = jnp.concatenate([own_pot[:, x * G : (x + 1) * G] for x in range(2)], axis=0)
            pot_high, pot_low = split(own_pot)
            line_send[...] = (dot(landing, pot_high) + dot(landing, pot_low)).reshape(ROWS, CAP, G)
            each_peer(lambda far_group, far_dom: back_copy(far_group, far_dom).start())
            back_ref[me] = line_send[me]
        potential = left_const(square(1), lines)
        for x in range(2):
            own = potential[:, x * G : (x + 1) * G]
            rho[x] = rho[x] - MIX_RATE * (rho[x] + sus[x] * (own + ion[x]))
        for h in range(2):
            core_copy(slot, h).wait_send()

    row_u = 1.0 + 2.0 * (iota((G, G), 0).astype(F32) + 0.5) / G
    lane_u = 1.0 + 2.0 * (iota((G, G), 1).astype(F32) + 0.5) / G
    x_u = [1.0 + 2.0 * ((2 * me + x).astype(F32) + 0.5) / G for x in range(2)]
    weighted = rho[0] * x_u[0] + rho[1] * x_u[1]
    plain = rho[0] + rho[1]
    sums = [weighted, plain * row_u, weighted * row_u, plain * lane_u]
    own_moments = jnp.zeros((1, G), F32)
    for index, term in enumerate(sums):
        value = jnp.sum(jnp.sum(term, axis=0, keepdims=True), axis=1, keepdims=True)
        own_moments = jnp.where(iota((1, G), 1) == index, value, own_moments)
    moment_send[...] = own_moments
    each_peer(lambda far_group, far_dom: moment_copy(far_group, far_dom).start())
    moment_recv[pl.ds(me, 1), :] = own_moments
    for x in range(2):
        pot_buf[x] = own_pot[x * 32 : (x + 1) * 32]
    stores = [
        pltpu.make_async_copy(pot_buf, pot_out, out_sems.at[0]),
        pltpu.make_async_copy(rho.at[:, columns, :], rho_out, out_sems.at[1]),
    ]
    for copy in stores:
        copy.start()
    lax.fori_loop(done, TILES, own_tile, 0)
    spot_iota = iota((G, atoms), 0)
    for corner in range(8):
        spot = lax.rem(cells[corner : corner + 1, :], G)
        weight_table[corner] = jnp.where(spot_iota == spot, weights[corner : corner + 1, :], 0.0)

    all_lines().wait_send()
    for k in (1, 2, 3):
        for index in range(3):
            slab_copy(index, k).wait_send()
        mm_copy(k).wait_send()
    fwd_all().wait_send()
    ret_all((ITERS - 1) % 2).wait_send()
    all_of(moment_recv.at[pl.ds(0, ROWS - 1)], moment_sems.at[0], moment_sems.at[1]).wait()
    all_of(back_ref.at[pl.ds(0, ROWS - 1)], back_sems.at[0], back_sems.at[1]).wait()

    back_high, back_low = split(back_ref[...].reshape(ROWS * CAP, G))
    values_high, values_low = split((dot(pick_t, back_high) + dot(pick_t, back_low)).T)
    values = jnp.concatenate([values_high, values_low], axis=0)
    moments = jnp.sum(moment_recv[...], axis=0, keepdims=True) * (1.0 / (G * math.sqrt(G)))
    moment = [
        jnp.sum(jnp.where(iota((1, G), 1) == m, moments, 0.0), axis=1, keepdims=True)
        for m in range(4)
    ]

    parts = []
    for start in range(0, atoms, 256):
        where = slice(start, start + 256)
        found = jnp.zeros((G, 256), F32)
        for corner in range(8):
            both = dot(values, line_table[corner, :, where])
            found = found + weight_table[corner, :, where] * (both[:G] + both[G:])
        parts.append(jnp.sum(found, axis=0, keepdims=True))
    total = short[...] + jnp.concatenate(parts, axis=1)
    for m in range(4):
        total = total + moment[m] * basis_ref[m : m + 1, :]
    mm_out[...] = jnp.where(lax.div(iota((1, atoms), 1), TILE) < live, total, 0.0)
    for copy in stores:
        copy.wait()


def copy_kernel(*refs):
    for source, target in zip(refs[:3], refs[3:]):
        target[...] = source[...]


def shards(
    atom_positions, atom_charges, multipole_basis, spread_cell, spread_weight, line_slab,
    line_target, neighbour_tiles, live_tiles, initial_density, susceptibility, ion_potential,
):
    vmem = pl.BlockSpec(memory_space=pltpu.VMEM)
    hbm = pl.BlockSpec(memory_space=pltpu.HBM)
    atoms = TILES * TILE
    square, big, flat = (jnp.asarray(table) for table in tables())
    block = initial_density.shape
    dma = pltpu.SemaphoreType.DMA
    buffer = pltpu.VMEM
    potential, density, values = pl.pallas_call(
        kernel,
        out_shape=(
            jax.ShapeDtypeStruct(block, F32),
            jax.ShapeDtypeStruct(block, F32),
            jax.ShapeDtypeStruct((1, atoms), F32),
        ),
        in_specs=[pl.BlockSpec(memory_space=pltpu.SMEM)] + [hbm] * 14,
        out_specs=(hbm, hbm, vmem),
        scratch_shapes=[
            buffer((8, atoms), jnp.int32),
            buffer((8, atoms), F32),
            buffer((TILES, TILE), F32),
            buffer((1, NLINES), jnp.int32),
            buffer((1, NLINES), jnp.int32),
            buffer((4, atoms), F32),
            buffer(square.shape, BF16),
            buffer(big.shape, BF16),
            buffer(flat.shape, F32),
            buffer((ROWS, 16, G), F32),
            buffer((ROWS, 16, G), F32),
            buffer((9, 4 * TILES, TILE), F32),
            buffer((2, G, G), F32),
            buffer((2, G, G), F32),
            buffer((2, G, G), F32),
            buffer((2, G, G), F32),
            buffer((2, ROWS, G), F32),
            buffer((ROWS, G), F32),
            buffer((2 * ROWS, G), F32),
            buffer((2, 2, 2, 2, 32, G), F32),
            buffer((G, G), F32),
            buffer((ROWS, CAP, G), F32),
            buffer((1, G), F32),
            buffer((ROWS, G), F32),
            buffer((ROWS, CAP, G), F32),
            buffer((3, TILE, TILES), F32),
            buffer((1, atoms), F32),
            dma((14,)),
            dma((2,)),
            dma((2, 3, 3)),
            dma((2, 3)),
            dma((9,)),
            dma((9,)),
            dma((2,)),
            dma((3,)),
            dma((2, 2, 2)),
            dma((2,)),
            dma((2,)),
            buffer((8, NLINES, atoms), BF16),
            buffer((8, G, atoms), F32),
            buffer((2, 32, G), F32),
            dma((2,)),
            pltpu.SMEM((TILES, NBR), jnp.int32),
        ],
        compiler_params=pltpu.CompilerParams(
            collective_id=0, has_side_effects=True, vmem_limit_bytes=VMEM_LIMIT
        ),
        name="embed",
    )(
        live_tiles, neighbour_tiles[0, 0], spread_cell[0, 0], spread_weight[0, 0],
        atom_positions.reshape(3 * TILES, TILE), atom_charges.reshape(TILES, TILE),
        line_slab.reshape(1, NLINES), line_target[0], initial_density, susceptibility,
        ion_potential, multipole_basis[0, 0], square, big, flat,
    )
    results = (potential, density, values)
    potential, density, values = pl.pallas_call(
        copy_kernel,
        out_shape=tuple(jax.ShapeDtypeStruct(r.shape, F32) for r in results),
        in_specs=[vmem] * 3,
        out_specs=(vmem,) * 3,
        name="results",
    )(*results)
    return potential, density, values[None]


def solution(mesh):
    row = ("group", "dom")
    placed = (
        P(row, "pen", None, None),
        P(row, "pen", None),
        P(row, "pen", None, None),
        P(row, "pen", None, None),
        P(row, "pen", None, None),
        P(row, "pen", None, None),
        P(row, "pen", None),
        P(row, "pen", None, None),
        P(row, "pen"),
        P(row, "pen", None),
        P(row, "pen", None),
        P(row, "pen", None),
    )
    return jax.shard_map(
        shards,
        mesh=mesh,
        in_specs=placed,
        out_specs=(P(row, "pen", None), P(row, "pen", None), P(row, "pen", None)),
        check_vma=False,
    )
```

```python
import math

import jax
import jax.numpy as jnp
import ml_dtypes
import numpy as np
from jax import lax
from jax.experimental import pallas as pl
from jax.experimental.pallas import tpu as pltpu
from jax.sharding import PartitionSpec as P

MESH = pl.DeviceIdType.MESH
F32 = jnp.float32
BF16 = jnp.bfloat16
G = 128
TILE = 128
TILES = 16
NBR = 16
ITERS = 4
ROWS = 64
PEN = 4
CAP = 8
NLINES = 256
MIX_RATE = 0.3
SCREENING = 0.1
BOX_HEIGHT = 4.0
SOFTENING = 0.01
ERF_SHIFT = 1.35
ERF_POLY = (
    8.048848463632075e-05,
    0.279831566396696,
    0.40782855654035,
    0.3006583844815809,
    1.260144403309312,
    -1.158323294058104,
    2.9062706842895354,
    -1.262709002135607,
)
VMEM_LIMIT = 64 * 1024 * 1024


def halves(table):
    high = table.astype(ml_dtypes.bfloat16)
    low = (table - high.astype(np.float64)).astype(ml_dtypes.bfloat16)
    return [high, low]


def tables():
    k = np.arange(G)
    angle = 2.0 * np.pi * (np.outer(k, k) % G) / G
    cas = (np.cos(angle) + np.sin(angle)) / np.sqrt(G)
    order = np.concatenate([np.arange(32) + 32 * (2 * z + c) for c in range(2) for z in range(2)])
    split_x = np.concatenate([np.arange(ROWS) * 2, np.arange(ROWS) * 2 + 1])
    square = halves(cas) + halves(cas[:, order]) + halves(cas[:, split_x]) + halves(cas[split_x, :])
    wide = np.zeros((2, G, 2, 2, ROWS))
    for x in range(2):
        for h in range(2):
            wide[x, :, h, x, :] = cas[:, h * ROWS : (h + 1) * ROWS]
    wide = wide.reshape(2 * G, 2 * G)
    big = halves(wide) + halves(wide.T)
    lam = 2.0 - 2.0 * np.cos(2.0 * np.pi * k / G)
    lam_rows = np.repeat(lam[:, None], G, axis=1)
    lam_lanes = np.zeros((8, G))
    for h in range(2):
        lam_lanes[h] = np.tile(lam[h * ROWS : (h + 1) * ROWS], 2)
    flat = np.concatenate([lam_rows, lam_lanes]).astype(np.float32)
    big = [part[:, h * G : (h + 1) * G] for part in big for h in range(2)]
    return np.stack(square), np.stack(big), flat


def split(x):
    high = x.astype(BF16)
    return high, (x - high.astype(F32)).astype(BF16)


def dot(a, b):
    return jnp.dot(a, b, preferred_element_type=F32)


def dot_nt(a, b):
    return lax.dot_general(a, b, (((1,), (1,)), ((), ())), preferred_element_type=F32)


def dot_tn(a, b):
    return lax.dot_general(a, b, (((0,), (0,)), ((), ())), preferred_element_type=F32)


def left_const(both, x):
    rows = both.shape[0] // 2
    x_high, x_low = split(x)
    wide = dot(both, x_high)
    return wide[:rows] + (wide[rows:] + dot(both[:rows], x_low))


def right_const(x, high, low):
    rows = x.shape[0]
    x_high, x_low = split(x)
    wide = dot(jnp.concatenate([x_high, x_low], axis=0), high)
    return wide[:rows] + (wide[rows:] + dot(x_high, low))


def iota(shape, dim):
    return lax.broadcasted_iota(jnp.int32, shape, dim)


FWD_TILES = (2, 2, 2, 2)
RET_TILES = (2, 2, 2, 1)


def pair_values(own, partner):
    dx = own[0] - partner[0]
    dy = own[1] - partner[1]
    dz = own[2] - partner[2]
    s = dx * dx + dy * dy + dz * dz + SOFTENING
    u = lax.rsqrt(s)
    t = 1.0 / (s * u + ERF_SHIFT)
    poly = jnp.full_like(t, ERF_POLY[-1])
    for coefficient in ERF_POLY[-2::-1]:
        poly = poly * t + coefficient
    return (partner[3] * u) * (poly * jnp.exp(-4.0 * s))


def kernel(
    live_ref, nbr_hbm, cell_hbm, weight_hbm, positions_hbm, charge_hbm, slab_hbm, target_hbm,
    rho_hbm, sus_hbm, ion_hbm, basis_hbm, square_hbm, big_hbm, flat_hbm,
    pot_out, rho_out, mm_out,
    cells, weights, charges, slab_buf, target_buf, basis_ref, square_ref, big_ref, flat_ref,
    send_ref, line_buf, halo_ref, mm, rho, sus, ion, fwd_send, fwd_recv, ret_send, ret_recv,
    green, line_send, moment_send, moment_recv, back_ref, columns_of, short,
    load_sems, line_sems, pen_sems, mm_sems, halo_send_sems, halo_recv_sems, fwd_sems, ret_sems,
    back_sems, moment_sems, line_table, weight_table, pot_buf, out_sems,
    nbr_ref,
):
    group, dom, pen = lax.axis_index("group"), lax.axis_index("dom"), lax.axis_index("pen")
    me = group * 16 + dom
    core, z_lo = lax.rem(pen, 2), pen // 2
    other_chip = lax.rem(pen + 2, PEN)
    sibling = z_lo * 2 + (1 - core)
    columns = pl.ds(pl.multiple_of(pen * 32, 32), 32)
    atoms = TILES * TILE

    first = [
        pltpu.make_async_copy(source, target, load_sems.at[index])
        for index, (source, target) in enumerate(
            (
                (cell_hbm, cells),
                (weight_hbm, weights),
                (charge_hbm, charges),
                (slab_hbm, slab_buf),
                (target_hbm, target_buf),
                (positions_hbm, halo_ref.at[4, pl.ds(0, 3 * TILES)]),
            )
        )
    ]
    later = [
        pltpu.make_async_copy(source, target, load_sems.at[6 + index])
        for index, (source, target) in enumerate(
            (
                (rho_hbm, rho.at[:, columns, :]),
                (sus_hbm, sus.at[:, columns, :]),
                (ion_hbm, ion.at[:, columns, :]),
                (flat_hbm, flat_ref),
                (square_hbm, square_ref),
                (big_hbm, big_ref),
                (basis_hbm, basis_ref),
                (nbr_hbm, nbr_ref),
            )
        )
    ]
    for copy in first:
        copy.start()

    def remote(src, dst, send_sem, recv_sem, where):
        return pltpu.make_async_remote_copy(
            src_ref=src, dst_ref=dst, send_sem=send_sem, recv_sem=recv_sem,
            device_id=where, device_id_type=MESH,
        )

    def ring(q):
        return lax.rem(2 + 3 * q + (q // 2) * (2 * q - 1), 4)

    dom_x, dom_y = dom // 4, lax.rem(dom, 4)
    offsets = (2, 1, 3, 0)
    doms = [
        lax.rem(dom_x + x, 4) * 4 + lax.rem(dom_y + y, 4) for x in offsets for y in offsets
    ]

    def each_peer(act):
        def step(q, carry):
            far_group = lax.rem(group + ring(q), 4)
            for far_dom in doms:
                act(far_group, far_dom)
            return carry

        lax.fori_loop(0, 3, step, 0)
        for far_dom in doms[:15]:
            act(group, far_dom)

    barrier = pltpu.get_barrier_semaphore()

    def signal(*where):
        pl.semaphore_signal(barrier, inc=1, device_id=where, device_id_type=MESH)

    def greet(far_group, far_dom):
        signal(far_group, far_dom, pen)
        for k in (2, 1, 3):
            signal(far_group, far_dom, lax.rem(pen + k, PEN))

    each_peer(greet)
    for k in (1, 2, 3):
        signal(group, dom, lax.rem(pen + k, PEN))
    for copy in later:
        copy.start()

    for copy in first:
        copy.wait()
    live = live_ref[0, 0]
    halo_ref[4, 3 * TILES :, :] = jnp.where(iota((TILES, TILE), 0) < live, charges[...], 0.0)
    slab_row = slab_buf[...]
    slab_rows = slab_row.astype(F32)
    slab_cols = jnp.concatenate(
        [
            jnp.broadcast_to(slab_rows[:, half * G : (half + 1) * G], (G, G)).T
            for half in range(2)
        ],
        axis=0,
    )
    slab_cols = jnp.concatenate([slab_cols, slab_cols], axis=1)
    same = (slab_cols == slab_rows) & (iota((NLINES, NLINES), 0) < iota((NLINES, NLINES), 1))
    rank = jnp.sum(same.astype(F32), axis=0, keepdims=True).astype(jnp.int32)
    pick = (iota((ROWS * CAP, NLINES), 0) == slab_row * CAP + rank).astype(F32)
    pick_high = pick.astype(BF16)
    owner = jnp.where(iota((ROWS, NLINES), 0) == slab_row, target_buf[...].astype(F32), 0.0)
    place = (iota((TILE, NLINES), 0) == rank).astype(F32)
    one, zero = jnp.ones((), BF16), jnp.zeros((), BF16)
    line_iota = iota((NLINES, atoms), 0).astype(F32).astype(BF16)
    cell_iota = iota((G, atoms), 0).astype(F32).astype(BF16)
    charge = jnp.concatenate(
        [halo_ref[4, 3 * TILES + t : 3 * TILES + t + 1, :] for t in range(TILES)], axis=1
    )

    def lines_of(corner):
        cell = cells[corner : corner + 1, :]
        line = lax.div(cell, G).astype(F32).astype(BF16)
        return cell, jnp.where(line_iota == line, one, zero)

    total = jnp.zeros((2 * G, NLINES), F32)
    for corner in range(8):
        cell, lines = lines_of(corner)
        line_table[corner] = lines
        high, low = split(weights[corner : corner + 1, :] * charge)
        hit = cell_iota == lax.rem(cell, G).astype(F32).astype(BF16)
        spots = jnp.concatenate([jnp.where(hit, high, zero), jnp.where(hit, low, zero)], axis=0)
        total = total + dot_nt(spots, lines)
    lines_high, lines_low = split(total[:G] + total[G:])
    send_ref[:, :CAP, :] = (dot_nt(pick_high, lines_high) + dot_nt(pick_high, lines_low)).reshape(
        ROWS, CAP, G
    )
    send_ref[:, CAP, :] = dot_nt(owner.astype(BF16), place.astype(BF16))

    pl.semaphore_wait(barrier, PEN * ROWS - 1)

    def send_lines(far_group, far_dom):
        remote(
            send_ref.at[far_group * 16 + far_dom, pl.ds(0, CAP + 1)],
            line_buf.at[me, pl.ds(0, CAP + 1)],
            line_sems.at[0], line_sems.at[1], (far_group, far_dom, pen),
        ).start()

    each_peer(send_lines)
    line_buf[me, 0 : CAP + 1, :] = send_ref[me, 0 : CAP + 1, :]

    slabs = ((rho_hbm, rho), (sus_hbm, sus), (ion_hbm, ion))

    def slab_copy(index, k):
        source, whole = slabs[index]
        return remote(
            source, whole.at[:, columns, :],
            pen_sems.at[0, index, k - 1], pen_sems.at[1, index, k - 1],
            (group, dom, lax.rem(pen + k, PEN)),
        )

    for k in (1, 2, 3):
        slab_copy(0, k).start()

    neighbours = [(dx, dy) for dx in (-1, 0, 1) for dy in (-1, 0, 1) if (dx, dy) != (0, 0)]

    def halo_copy(dx, dy):
        number = (1 - dx) * 3 + 1 - dy
        row = lax.rem(me + dx + ROWS, ROWS)
        return remote(
            halo_ref.at[4], halo_ref.at[number], halo_send_sems.at[number],
            halo_recv_sems.at[number],
            (row // 16, lax.rem(row, 16), lax.rem(pen + dy + PEN, PEN)),
        )

    for dx, dy in neighbours:
        halo_copy(dx, dy).start()
    for copy in later:
        copy.wait()

    half = me // 32
    y_row = pen * 32 + lax.rem(me, 32)
    lam_yz = flat_ref[pl.ds(y_row, 1), :] + flat_ref[pl.ds(G + half, 1), :]
    green[...] = 1.0 / (SCREENING + (flat_ref[0:G, :] + lam_yz))

    pick_t = pick.T.astype(BF16)

    source_of = iota((ROWS * CAP, ROWS), 0) // CAP == iota((ROWS * CAP, ROWS), 1)
    source_of = source_of.astype(F32).astype(BF16)
    own_lane = iota((ROWS * CAP, G), 1) == lax.rem(iota((ROWS * CAP, G), 0), CAP)
    for axis in range(3):
        columns_of[axis] = halo_ref[4, axis * TILES : (axis + 1) * TILES, :].T * (
            BOX_HEIGHT if axis == 2 else 1.0
        )

    def all_of(ref, send_sem, recv_sem):
        return remote(ref, ref, send_sem, recv_sem, (group, dom, sibling))

    def all_lines():
        most = line_buf.at[pl.ds(0, ROWS - 1), pl.ds(0, CAP + 1)]
        return all_of(most, line_sems.at[0], line_sems.at[1])

    all_lines().wait_recv()
    targets = line_buf[:, CAP, :]
    targets_t = jnp.concatenate([targets, targets], axis=0).T
    line_of_row = iota((ROWS, ROWS), 0).astype(F32)
    landing_t = jnp.concatenate(
        [(targets_t[k : k + 1, :ROWS] == line_of_row).astype(F32) for k in range(CAP)], axis=1
    ).astype(BF16)
    received = jnp.concatenate([line_buf[:, k, :] for k in range(CAP)], axis=0)
    lines_high, lines_low = split(received)
    own_mm = dot(landing_t, lines_high) + dot(landing_t, lines_low)
    for x in range(2):
        mm[x, columns, :] = own_mm[x * 32 : (x + 1) * 32]

    def mm_copy(k):
        return remote(
            mm.at[:, columns, :], mm.at[:, columns, :], mm_sems.at[0, k - 1], mm_sems.at[1, k - 1],
            (group, dom, lax.rem(pen + k, PEN)),
        )

    for k in (1, 2, 3):
        mm_copy(k).start()
    spread_targets = dot(source_of, targets.astype(BF16))
    target = jnp.sum(jnp.where(own_lane, spread_targets, 0.0), axis=1, keepdims=True)
    landing = (target == iota((ROWS * CAP, ROWS), 1).astype(F32)).astype(F32).astype(BF16)
    tile_lane = iota((TILE, TILES), 1)

    def own_tile(t, carry):
        own = [
            jnp.broadcast_to(
                jnp.sum(jnp.where(tile_lane == t, columns_of[axis], 0.0), axis=1, keepdims=True),
                (TILE, TILE),
            )
            for axis in range(3)
        ]

        def partner_tile(n, total):
            chosen = nbr_ref[t, n]
            d = lax.div(chosen, TILES)
            tile = lax.rem(chosen, TILES)
            row = [halo_ref[d, pl.ds(axis * TILES + tile, 1), :] for axis in range(4)]
            row[0] = row[0] + (lax.div(d, 3) - 1).astype(F32)
            row[1] = row[1] + (lax.rem(d, 3) - 1).astype(F32)
            row[2] = row[2] * BOX_HEIGHT
            return total + pair_values(own, row)

        total = lax.fori_loop(0, NBR, partner_tile, jnp.zeros((TILE, TILE), F32))
        short[:, pl.ds(pl.multiple_of(t * TILE, TILE), TILE)] = jnp.sum(
            total.T, axis=0, keepdims=True
        )
        return carry

    for dx, dy in neighbours:
        halo_copy(dx, dy).wait()
    for dx, dy in neighbours:
        outside = (me + dx < 0) | (me + dx >= ROWS) | (pen + dy < 0) | (pen + dy >= PEN)

        @pl.when(outside)
        def _():
            halo_ref[(dx + 1) * 3 + dy + 1] = jnp.zeros((4 * TILES, TILE), F32)

    done = 0
    for k in (1, 2, 3):
        slab_copy(0, k).wait_recv()
    for k in (1, 2, 3):
        mm_copy(k).wait_recv()

    def square(index):
        return jnp.concatenate([square_ref[2 * index], square_ref[2 * index + 1]], axis=0)

    def wide(index):
        return jnp.concatenate([big_ref[2 * index], big_ref[2 * index + 1]], axis=1)

    low_lanes = iota((ROWS, G), 1) < ROWS

    y_rows = [pl.ds(pl.multiple_of((2 * z + core) * 32, 32), 32) for z in range(2)]
    y_table = jnp.concatenate([square_ref[part, rows, :] for part in range(2) for rows in y_rows])
    across, beside = lax.rem(group + 2, 4), lax.rem(group + 3 - 2 * z_lo, 4)

    def fwd_copy(far_group, far_dom, z):
        return remote(
            fwd_send.at[z, pl.ds(far_group * 16 + far_dom, 1)], fwd_recv.at[pl.ds(me, 1)],
            fwd_sems.at[0], fwd_sems.at[1], (far_group, far_dom, 2 * z + core),
        )

    def fwd_all():
        return all_of(fwd_recv.at[pl.ds(0, ROWS - 1)], fwd_sems.at[0], fwd_sems.at[1])

    def ret_copy(slot, far_group, far_dom, column):
        return remote(
            ret_send.at[pl.ds(far_group * 16 + far_dom, 1)],
            ret_recv.at[slot, half, core, z_lo, pl.ds(lax.rem(me, 32), 1)],
            ret_sems.at[0], ret_sems.at[1 + slot], (far_group, far_dom, column),
        )

    def ret_all(slot):
        return all_of(ret_send.at[pl.ds(0, PEN * ROWS - 1)], ret_sems.at[0], ret_sems.at[1 + slot])

    def back_copy(far_group, far_dom):
        return remote(
            line_send.at[far_group * 16 + far_dom], back_ref.at[me],
            back_sems.at[0], back_sems.at[1], (far_group, far_dom, pen),
        )

    def moment_copy(far_group, far_dom):
        return remote(
            moment_send, moment_recv.at[pl.ds(me, 1)],
            moment_sems.at[0], moment_sems.at[1], (far_group, far_dom, pen),
        )

    for iteration in range(ITERS):
        slot = iteration % 2
        source = jnp.concatenate([rho[0] + mm[0], rho[1] + mm[1]], axis=1)
        spectrum = right_const(left_const(y_table, source), wide(0), wide(1))
        if iteration > 0:
            fwd_all().wait_send()
        for z in range(2):
            for h in range(2):
                fwd_send[z, h * 32 : (h + 1) * 32, :] = spectrum[
                    z * 32 : (z + 1) * 32, h * G : (h + 1) * G
                ]

        def send_across(far_dom):
            fwd_copy(across, far_dom, 1 - z_lo).start()

        def send_beside(far_dom):
            fwd_copy(beside, far_dom, 1 - z_lo).start()
            fwd_copy(beside, far_dom, z_lo).start()

        def send_near(far_dom):
            fwd_copy(group, far_dom, z_lo).start()

        for far_dom in doms:
            send_across(far_dom)
        for far_dom in doms:
            send_beside(far_dom)
        for far_dom in doms[:15]:
            send_near(far_dom)
        fwd_recv[pl.ds(me, 1), :] = fwd_send[z_lo, pl.ds(me, 1), :]
        if iteration == 0:
            for index in (1, 2):
                for k in (1, 2, 3):
                    slab_copy(index, k).start()
        lax.fori_loop(done, done + FWD_TILES[iteration], own_tile, 0)
        done += FWD_TILES[iteration]
        fwd_all().wait_recv()
        received = fwd_recv[...]
        both = jnp.concatenate([received, pltpu.roll(received, ROWS, 1)], axis=0)
        modes = left_const(square(2), both) * green[...]
        solved = left_const(square(3), modes)
        if iteration > 0:
            ret_all(1 - slot).wait_send()
        ret_send[:ROWS, :] = jnp.where(low_lanes, solved[:ROWS], pltpu.roll(solved[ROWS:], ROWS, 1))

        def send_ret(far_group, far_dom):
            for k in (2, 3, 1, 0):
                ret_copy(slot, far_group, far_dom, lax.rem(pen + k, PEN)).start()

        each_peer(send_ret)
        for k in (2, 3, 1):
            ret_copy(slot, group, dom, lax.rem(pen + k, PEN)).start()
        ret_recv[slot, half, core, z_lo, pl.ds(lax.rem(me, 32), 1)] = ret_send[pl.ds(me, 1), :]
        lax.fori_loop(done, done + RET_TILES[iteration], own_tile, 0)
        done += RET_TILES[iteration]
        ret_all(slot).wait_recv()
        if iteration == 0:
            for index in (1, 2):
                for k in (1, 2, 3):
                    slab_copy(index, k).wait_recv()
        lines = jnp.concatenate([ret_recv[slot, h].reshape(G, G) for h in range(2)], axis=1)
        lines = right_const(lines, wide(2), wide(3))
        if iteration == ITERS - 1:
            own_table = jnp.concatenate([square_ref[part, columns, :] for part in (2, 3)])
            own_pot = left_const(own_table, lines)
            own_pot = jnp.concatenate([own_pot[:, x * G : (x + 1) * G] for x in range(2)], axis=0)
            pot_high, pot_low = split(own_pot)
            line_send[...] = (dot(landing, pot_high) + dot(landing, pot_low)).reshape(ROWS, CAP, G)
            each_peer(lambda far_group, far_dom: back_copy(far_group, far_dom).start())
            back_ref[me] = line_send[me]
        potential = left_const(square(1), lines)
        for x in range(2):
            own = potential[:, x * G : (x + 1) * G]
            rho[x] = rho[x] - MIX_RATE * (rho[x] + sus[x] * (own + ion[x]))

    row_u = 1.0 + 2.0 * (iota((G, G), 0).astype(F32) + 0.5) / G
    lane_u = 1.0 + 2.0 * (iota((G, G), 1).astype(F32) + 0.5) / G
    x_u = [1.0 + 2.0 * ((2 * me + x).astype(F32) + 0.5) / G for x in range(2)]
    weighted = rho[0] * x_u[0] + rho[1] * x_u[1]
    plain = rho[0] + rho[1]
    sums = [weighted, plain * row_u, weighted * row_u, plain * lane_u]
    own_moments = jnp.zeros((1, G), F32)
    for index, term in enumerate(sums):
        value = jnp.sum(jnp.sum(term, axis=0, keepdims=True), axis=1, keepdims=True)
        own_moments = jnp.where(iota((1, G), 1) == index, value, own_moments)
    moment_send[...] = own_moments
    each_peer(lambda far_group, far_dom: moment_copy(far_group, far_dom).start())
    moment_recv[pl.ds(me, 1), :] = own_moments
    for x in range(2):
        pot_buf[x] = own_pot[x * 32 : (x + 1) * 32]
    stores = [
        pltpu.make_async_copy(pot_buf, pot_out, out_sems.at[0]),
        pltpu.make_async_copy(rho.at[:, columns, :], rho_out, out_sems.at[1]),
    ]
    for copy in stores:
        copy.start()
    lax.fori_loop(done, TILES, own_tile, 0)
    spot_iota = iota((G, atoms), 0)
    for corner in range(8):
        spot = lax.rem(cells[corner : corner + 1, :], G)
        weight_table[corner] = jnp.where(spot_iota == spot, weights[corner : corner + 1, :], 0.0)

    all_lines().wait_send()
    for k in (1, 2, 3):
        for index in range(3):
            slab_copy(index, k).wait_send()
        mm_copy(k).wait_send()
    fwd_all().wait_send()
    ret_all((ITERS - 1) % 2).wait_send()
    all_of(moment_recv.at[pl.ds(0, ROWS - 1)], moment_sems.at[0], moment_sems.at[1]).wait()
    all_of(back_ref.at[pl.ds(0, ROWS - 1)], back_sems.at[0], back_sems.at[1]).wait()

    back_high, back_low = split(back_ref[...].reshape(ROWS * CAP, G))
    values_high, values_low = split((dot(pick_t, back_high) + dot(pick_t, back_low)).T)
    values = jnp.concatenate([values_high, values_low], axis=0)
    moments = jnp.sum(moment_recv[...], axis=0, keepdims=True) * (1.0 / (G * math.sqrt(G)))
    moment = [
        jnp.sum(jnp.where(iota((1, G), 1) == m, moments, 0.0), axis=1, keepdims=True)
        for m in range(4)
    ]

    parts = []
    for start in range(0, atoms, 256):
        where = slice(start, start + 256)
        found = jnp.zeros((G, 256), F32)
        for corner in range(8):
            both = dot(values, line_table[corner, :, where])
            found = found + weight_table[corner, :, where] * (both[:G] + both[G:])
        parts.append(jnp.sum(found, axis=0, keepdims=True))
    total = short[...] + jnp.concatenate(parts, axis=1)
    for m in range(4):
        total = total + moment[m] * basis_ref[m : m + 1, :]
    mm_out[...] = jnp.where(lax.div(iota((1, atoms), 1), TILE) < live, total, 0.0)
    for copy in stores:
        copy.wait()


def copy_kernel(*refs):
    for source, target in zip(refs[:3], refs[3:]):
        target[...] = source[...]


def shards(
    atom_positions, atom_charges, multipole_basis, spread_cell, spread_weight, line_slab,
    line_target, neighbour_tiles, live_tiles, initial_density, susceptibility, ion_potential,
):
    vmem = pl.BlockSpec(memory_space=pltpu.VMEM)
    hbm = pl.BlockSpec(memory_space=pltpu.HBM)
    atoms = TILES * TILE
    square, big, flat = (jnp.asarray(table) for table in tables())
    block = initial_density.shape
    dma = pltpu.SemaphoreType.DMA
    buffer = pltpu.VMEM
    potential, density, values = pl.pallas_call(
        kernel,
        out_shape=(
            jax.ShapeDtypeStruct(block, F32),
            jax.ShapeDtypeStruct(block, F32),
            jax.ShapeDtypeStruct((1, atoms), F32),
        ),
        in_specs=[pl.BlockSpec(memory_space=pltpu.SMEM)] + [hbm] * 14,
        out_specs=(hbm, hbm, vmem),
        scratch_shapes=[
            buffer((8, atoms), jnp.int32),
            buffer((8, atoms), F32),
            buffer((TILES, TILE), F32),
            buffer((1, NLINES), jnp.int32),
            buffer((1, NLINES), jnp.int32),
            buffer((4, atoms), F32),
            buffer(square.shape, BF16),
            buffer(big.shape, BF16),
            buffer(flat.shape, F32),
            buffer((ROWS, 16, G), F32),
            buffer((ROWS, 16, G), F32),
            buffer((9, 4 * TILES, TILE), F32),
            buffer((2, G, G), F32),
            buffer((2, G, G), F32),
            buffer((2, G, G), F32),
            buffer((2, G, G), F32),
            buffer((2, ROWS, G), F32),
            buffer((ROWS, G), F32),
            buffer((PEN * ROWS, G), F32),
            buffer((2, 2, 2, 2, 32, G), F32),
            buffer((G, G), F32),
            buffer((ROWS, CAP, G), F32),
            buffer((1, G), F32),
            buffer((ROWS, G), F32),
            buffer((ROWS, CAP, G), F32),
            buffer((3, TILE, TILES), F32),
            buffer((1, atoms), F32),
            dma((14,)),
            dma((2,)),
            dma((2, 3, 3)),
            dma((2, 3)),
            dma((9,)),
            dma((9,)),
            dma((2,)),
            dma((3,)),
            dma((2,)),
            dma((2,)),
            buffer((8, NLINES, atoms), BF16),
            buffer((8, G, atoms), F32),
            buffer((2, 32, G), F32),
            dma((2,)),
            pltpu.SMEM((TILES, NBR), jnp.int32),
        ],
        compiler_params=pltpu.CompilerParams(
            collective_id=0, has_side_effects=True, vmem_limit_bytes=VMEM_LIMIT
        ),
        name="embed",
    )(
        live_tiles, neighbour_tiles[0, 0], spread_cell[0, 0], spread_weight[0, 0],
        atom_positions.reshape(3 * TILES, TILE), atom_charges.reshape(TILES, TILE),
        line_slab.reshape(1, NLINES), line_target[0], initial_density, susceptibility,
        ion_potential, multipole_basis[0, 0], square, big, flat,
    )
    results = (potential, density, values)
    potential, density, values = pl.pallas_call(
        copy_kernel,
        out_shape=tuple(jax.ShapeDtypeStruct(r.shape, F32) for r in results),
        in_specs=[vmem] * 3,
        out_specs=(vmem,) * 3,
        name="results",
    )(*results)
    return potential, density, values[None]


def solution(mesh):
    row = ("group", "dom")
    placed = (
        P(row, "pen", None, None),
        P(row, "pen", None),
        P(row, "pen", None, None),
        P(row, "pen", None, None),
        P(row, "pen", None, None),
        P(row, "pen", None, None),
        P(row, "pen", None),
        P(row, "pen", None, None),
        P(row, "pen"),
        P(row, "pen", None),
        P(row, "pen", None),
        P(row, "pen", None),
    )
    return jax.shard_map(
        shards,
        mesh=mesh,
        in_specs=placed,
        out_specs=(P(row, "pen", None), P(row, "pen", None), P(row, "pen", None)),
        check_vma=False,
    )
```
